256 devices in a mesh: row: 16 (over x, y), col: 16 (over z, core).
Axes of the slice: x: 4, y: 4, z: 8, core: 2. Of those that a mesh axis runs over, the one named last changes fastest.
Arguments:
- panel_index: int32 [1], replicated, may hold values from 0 to 127
- coords: float32 [2, 8, 16, 128], P(None, None, 'row'), may hold values from 0 to 1
- region_ids: int32 [8, 16, 128], P(None, 'row'), may hold values from 0 to 15
- nugget: float32 [16], replicated, may hold values from 2 to 8
- variance: float32 [1], replicated, may hold values from 1 to 4
- length: float32 [1], replicated, may hold values from 0.02 to 0.06
- correction: float32 [8, 16, 128, 8, 16, 128], P(None, 'row', None, None, 'col'), may hold values from -0.5 to 0.5, as said below
- bin_index: int32 [8, 16, 16, 8], P(None, 'row', 'col'), may hold values from 0 to 4095
- fraction: float32 [8, 16, 16, 8], P(None, 'row', 'col'), may hold values from 0.05 to 0.95
- weights: float32 [8, 16, 16, 8], P(None, 'row', 'col'), may hold values from 0.5 to 6
Outputs:
- trailing: float32 [8, 16, 128, 8, 16, 128], P(None, 'row', None, None, 'col')
- panel: float32 [8, 16, 128, 128], P(None, 'row')
- scores_out: float32 [8, 16, 128], P(None, 'row')
- likelihood_terms: float32 [2], replicated
The draws below stay inside these ranges and needn't reach their ends.
Inputs may be any that keep to these rules, and one draw needn't show every extreme that they name: correction is symmetric as a 16384 x 16384 matrix; in a diagonal tile (row tile equal to column tile) every entry has magnitude at most 0.015.
All inputs are finite; a program needn't handle non-finite values.
Results may differ from the reference program's by a relative error of at most 0.0003.
Values sent between devices are 32-bit elements; how exact they have to be, the bound alone decides.
A program may use at most 64 MiB of HBM per device.

```python
import math
import jax
import jax.numpy as jnp
from jax import lax

TILE = 128
NBINS = 4096
NREG = 16
NT = 128
NS = 16384
RT = 8
CT = 8
SUB = 8
N_ROW = 16
N_COL = 16


def draw_correction(key, part):
    key = jax.random.fold_in(key, 7)
    raw = jax.random.uniform(key, (NS, NS), jnp.float32, -1.0, 1.0)
    same_tile = lax.broadcasted_iota(jnp.int32, (NS, NS), 0) // TILE == lax.broadcasted_iota(jnp.int32, (NS, NS), 1) // TILE
    scale = jnp.where(same_tile, 0.015, 0.5)
    symmetric = 0.5 * (raw + raw.T)
    return (scale * symmetric).reshape(RT, N_ROW, TILE, CT, N_COL, TILE)


def draw_weights(key, part):
    key = jax.random.fold_in(key, 11)
    shape = (RT, N_ROW, N_COL, SUB)
    base = jnp.exp(jax.random.uniform(key, shape, jnp.float32, math.log(0.5), math.log(2.0)))
    device_rank = lax.broadcasted_iota(jnp.float32, shape, 1) * N_COL + lax.broadcasted_iota(jnp.float32, shape, 2)
    return base * (1.0 + 2.0 * device_rank / (N_ROW * N_COL - 1))


def plant(result, key, low, largest):
    longest = result.shape.index(max(result.shape))
    spots = []
    for shift in (0, 1):
        where = [jax.random.randint(jax.random.fold_in(key, axis), (), 0, length) for axis, length in enumerate(result.shape)]
        where[longest] = (where[longest] + shift) % result.shape[longest]
        spots.append(tuple(where))
    return result.at[spots[0]].set(low).at[spots[1]].set(largest)


def steps_of(stream_key, shape, shards, smallest, top_value):
    def one(axis_at, blocks):
        draws = jax.random.uniform(jax.random.fold_in(jax.random.fold_in(stream_key, 6), axis_at), (blocks,), jnp.float32, smallest / len(shards), top_value / len(shards))
        return jnp.repeat(jnp.exp(draws), shape[axis_at] // blocks).reshape((-1,) + (1,) * (len(shape) - axis_at - 1))

    factor_of = one(*shards[0])
    for cut in shards[1:]:
        factor_of = factor_of * one(*cut)
    return factor_of


def setup_inputs(seed: int = 0) -> dict:
    key_of = jax.random.split(jax.random.key(seed), 11)
    panel_index = jax.random.randint(key_of[0], (1,), 0, NT).astype(jnp.int32)
    coords = jnp.clip(1.0 * jax.random.uniform(key_of[1], (2, RT, N_ROW, TILE), jnp.float32) ** steps_of(key_of[1], (2, RT, N_ROW, TILE), ((2, 16),), -0.2, 0.2), 0.0, 1.0)
    region_ids = plant(jax.random.randint(key_of[2], (RT, N_ROW, TILE), 0, NREG), jax.random.fold_in(key_of[2], 1), 0, NREG - 1).astype(jnp.int32)
    nugget = jnp.clip(jnp.exp(jax.random.uniform(key_of[3], (NREG,), jnp.float32, math.log(2.0), math.log(8.0))), 2.0, 8.0)
    variance = jnp.clip(jnp.exp(jax.random.uniform(key_of[4], (1,), jnp.float32, math.log(1.0), math.log(4.0))), 1.0, 4.0)
    length = jnp.clip(jnp.exp(jax.random.uniform(key_of[5], (1,), jnp.float32, math.log(0.02), math.log(0.06))), 0.02, 0.06)
    correction = draw_correction(jax.random.fold_in(key_of[10], 71), 0)
    bin_index = plant(jax.random.randint(key_of[7], (RT, N_ROW, N_COL, SUB), 0, NBINS), jax.random.fold_in(key_of[7], 1), 0, NBINS - 1).astype(jnp.int32)
    fraction = jnp.clip(0.05 + 0.9 * jax.random.uniform(key_of[8], (RT, N_ROW, N_COL, SUB), jnp.float32) ** steps_of(key_of[8], (RT, N_ROW, N_COL, SUB), ((1, 16), (2, 16)), -0.2, 0.2), 0.05, 0.95)
    weights = draw_weights(jax.random.fold_in(key_of[10], 71), 0)
    return {"panel_index": panel_index, "coords": coords, "region_ids": region_ids, "nugget": nugget, "variance": variance, "length": length, "correction": correction, "bin_index": bin_index, "fraction": fraction, "weights": weights}


ROOT_THREE = 1.7320508075688772
ROOT_TWO = 1.4142135623730951
HIGH = lax.Precision.HIGHEST

def matern_kernel(first, second, variance, length):
    delta_x = first[0][:, None] - second[0][None, :]
    delta_y = first[1][:, None] - second[1][None, :]
    scaled = ROOT_THREE * jnp.sqrt(delta_x * delta_x + delta_y * delta_y) / length
    return variance * (1.0 + scaled) * jnp.exp(-scaled)

def reference(panel_index, coords, region_ids, nugget, variance, length, correction, bin_index, fraction, weights):
    pivot = panel_index[0]
    flat_bins = bin_index.reshape(-1)
    hist = jax.ops.segment_sum(weights.reshape(-1), flat_bins, num_segments=NBINS)
    total = jnp.sum(hist)
    before = jnp.cumsum(hist) - hist
    prob = (before[flat_bins] + fraction.reshape(-1) * hist[flat_bins]) / total
    scores = ROOT_TWO * lax.erf_inv(2.0 * jnp.clip(prob, 0.01, 0.99) - 1.0)
    sites = coords.reshape(2, NS)
    matrix = correction.reshape(NS, NS)
    nugget_site = nugget[region_ids.reshape(-1)]
    site_ids = jnp.arange(NS, dtype=jnp.int32)
    start = (pivot * TILE).astype(jnp.int32)
    pivot_sites = lax.dynamic_slice_in_dim(sites, start, TILE, 1)
    pivot_ids = lax.dynamic_slice_in_dim(site_ids, start, TILE, 0)
    column = matern_kernel(sites, pivot_sites, variance[0], length[0])
    column = column + jnp.where(site_ids[:, None] == pivot_ids[None, :], nugget_site[:, None], 0.0)
    column = column - lax.dynamic_slice_in_dim(matrix, start, TILE, 1)
    block = lax.dynamic_slice_in_dim(column, start, TILE, 0)
    factor = jnp.linalg.cholesky(block)
    panel = jax.scipy.linalg.solve_triangular(factor, column.T, lower=True).T
    solved = jax.scipy.linalg.solve_triangular(factor, lax.dynamic_slice_in_dim(scores, start, TILE, 0), lower=True)
    updated = scores - jnp.dot(panel, solved, precision=HIGH)
    updated = lax.dynamic_update_slice_in_dim(updated, solved, start, 0)

    def one_tile(index):
        row_start = (index * TILE).astype(jnp.int32)
        row_sites = lax.dynamic_slice_in_dim(sites, row_start, TILE, 1)
        row_ids = lax.dynamic_slice_in_dim(site_ids, row_start, TILE, 0)
        row_nugget = lax.dynamic_slice_in_dim(nugget_site, row_start, TILE, 0)
        row_panel = lax.dynamic_slice_in_dim(panel, row_start, TILE, 0)
        rows = matern_kernel(row_sites, sites, variance[0], length[0])
        rows = rows + jnp.where(row_ids[:, None] == site_ids[None, :], row_nugget[:, None], 0.0)
        rows = rows - lax.dynamic_slice_in_dim(matrix, row_start, TILE, 0)
        return rows - jnp.dot(row_panel, panel.T, precision=HIGH)
    trailing = lax.map(one_tile, jnp.arange(NT, dtype=jnp.int32))
    likelihood_terms = jnp.stack([2.0 * jnp.sum(jnp.log(jnp.diagonal(factor))), jnp.dot(solved, solved, precision=HIGH)])
    return (trailing.reshape(RT, N_ROW, TILE, CT, N_COL, TILE), panel.reshape(RT, N_ROW, TILE, TILE), updated.reshape(RT, N_ROW, TILE), likelihood_terms)
```

```python
import functools

import jax
import jax.numpy as jnp
from jax import lax
from jax.experimental import pallas as pl
from jax.experimental.pallas import tpu as pltpu
from jax.sharding import PartitionSpec as P

F32 = jnp.float32
BF16 = jnp.bfloat16
I32 = jnp.int32
MESH = pl.DeviceIdType.MESH
N = 16
NREG = 16
ROOT_THREE = 1.7320508075688772
ROOT_TWO = 1.4142135623730951
NT = (((1,), (1,)), ((), ()))
NN = (((1,), (0,)), ((), ()))
TN = (((0,), (0,)), ((), ()))
PIECE = 64
MIB = 2**20


def iota(shape, dim):
    return lax.broadcasted_iota(I32, shape, dim)


def split2(x):
    high = x.astype(BF16)
    return high, (x - high.astype(F32)).astype(BF16)


def split3(x):
    high = x.astype(BF16)
    rest = x - high.astype(F32)
    mid = rest.astype(BF16)
    return high, mid, (rest - mid.astype(F32)).astype(BF16)


def dot3(a, b, dims):
    (ca,), (cb,) = dims[0]
    ah, al = split2(a)
    bh, bl = split2(b)
    return lax.dot_general(
        jnp.concatenate([ah, ah, al], axis=ca),
        jnp.concatenate([bh, bl, bh], axis=cb),
        dims,
        preferred_element_type=F32,
    )


def matern(dx, dy, variance):
    scaled = jnp.sqrt(dx * dx + dy * dy)
    return (variance + variance * scaled) * jnp.exp(-scaled)


def factor_inverse(work, inv):
    nb = 16
    groups = nb // 8
    sub = iota((8, 128), 0)
    lane = iota((nb, 128), 1)
    inv[...] = (iota((128, 128), 0) == iota((128, 128), 1)).astype(F32)

    def block(p, carry):
        rows_k = [work[8 * g : 8 * g + 8, :] for g in range(groups)]
        rows_i = [inv[8 * g : 8 * g + 8, :] for g in range(groups)]
        col = [
            [
                jnp.broadcast_to(rows_k[g][:, q : q + 1], (8, 128)) if 8 * g + 7 >= q else None
                for g in range(groups)
            ]
            for q in range(nb)
        ]
        pivots = [jnp.ones((8, 128), F32) for _ in range(groups)]
        for j in range(nb):
            gj, sj = divmod(j, 8)
            pivot = jnp.broadcast_to(col[j][gj][sj : sj + 1, :], (8, 128))
            pivots[gj] = jnp.where(sub == sj, pivot, pivots[gj])
            if j == nb - 1:
                break
            recip = 1.0 / pivot
            mult = [None] * groups
            for g in range(gj, groups):
                m = col[j][g] * recip
                mult[g] = jnp.where(sub > sj, m, 0.0) if g == gj else m
            for q in range(j + 1, nb):
                gq, sq = divmod(q, 8)
                scale = jnp.broadcast_to(col[j][gq][sq : sq + 1, :], (8, 128))
                for g in range(gq, groups):
                    col[q][g] = col[q][g] - mult[g] * scale
            row_k = jnp.broadcast_to(rows_k[gj][sj : sj + 1, :], (8, 128))
            row_i = jnp.broadcast_to(rows_i[gj][sj : sj + 1, :], (8, 128))
            for g in range(gj, groups):
                if 8 * g + 7 > j:
                    rows_k[g] = rows_k[g] - mult[g] * row_k
                    rows_i[g] = rows_i[g] - mult[g] * row_i
        roots = [lax.rsqrt(x) for x in pivots]
        upper = jnp.concatenate([rows_k[g] * roots[g] for g in range(groups)], axis=0)
        done = jnp.concatenate([rows_i[g] * roots[g] for g in range(groups)], axis=0)
        below = jnp.where((lane >= nb) & (lane < 128 - nb * p), upper, 0.0)
        h, m, l = split3(below)
        h2, m2, l2 = split3(done)
        left = jnp.concatenate([h, h, m, m, h, l], axis=0)
        right = jnp.concatenate(
            [
                jnp.concatenate([h, m, h, m, l, h], axis=0),
                jnp.concatenate([h2, m2, h2, m2, l2, h2], axis=0),
            ],
            axis=1,
        )
        update = lax.dot_general(left, right, TN, preferred_element_type=F32)
        next_k = work[nb:, :] - update[nb:, :128]
        next_i = inv[nb:, :] - update[nb:, 128:]
        work[0 : 128 - nb, :] = pltpu.roll(next_k, 128 - nb, 1)
        inv[0 : 128 - nb, :] = next_i
        inv[128 - nb :, :] = done
        return carry

    lax.fori_loop(0, 128 // nb, block, 0)


def exchange_kernel(
    d,
    k_ref,
    nugget_ref,
    variance_ref,
    length_ref,
    coords_s,
    coords_ref,
    regions_ref,
    bins_ref,
    fraction_ref,
    weights_ref,
    corr_hbm,
    matrix_hbm,
    rows_out,
    cols_out,
    inverse_out,
    hist_out,
    sites_out,
    pivot_out,
    corr,
    row_raw,
    col_raw,
    work,
    inverse,
    factor_rx,
    col_sites,
    pivot_info,
    obs,
    hist,
    hist_rx,
    hist_all,
    sites,
    pivot_obs,
    in_sem,
    out_sem,
    send,
    recv,
    row_recv,
):
    r = lax.axis_index("row")
    c = lax.axis_index("col")
    sibling = c + 1 - 2 * lax.rem(c, 2)
    tile_at = jnp.full((128, 128), k_ref[0] // N, I32)
    (
        S_SITES, S_PIVOT, S_OBS, S_F1, S_F2, S_F3, S_H2, S_H3, S_PO, S_R1, S_R2, S_R3, S_C1, S_C2,
    ) = range(14)

    def row_peer(i):
        return lax.rem(r + i, N)

    def col_peer(i):
        return lax.rem(c + i, N)

    def send_to(src, dst, which, to, sem=None):
        pltpu.make_async_remote_copy(
            src_ref=src,
            dst_ref=dst,
            send_sem=send.at[which],
            recv_sem=recv.at[which] if sem is None else sem,
            device_id=to,
            device_id_type=MESH,
        ).start()

    def wait(ref, sem):
        pltpu.make_async_copy(ref, ref, sem).wait()

    def each_peer(body):
        def step(i, carry):
            body(i)
            return carry

        lax.fori_loop(1, N, step, 0)

    def rows8(ref, i):
        return ref.at[pl.ds(pl.multiple_of(i * 8, 8), 8)]

    def piece(ref, i):
        return ref.at[pl.ds(pl.multiple_of(i * PIECE, PIECE), PIECE)]

    barrier = pltpu.get_barrier_semaphore()

    def greet(i):
        pl.semaphore_signal(barrier, inc=1, device_id=(row_peer(i), c), device_id_type=MESH)
        pl.semaphore_signal(barrier, inc=1, device_id=(r, col_peer(i)), device_id_type=MESH)

    each_peer(greet)
    load = pltpu.make_async_copy(corr_hbm, corr, in_sem)
    load.start()

    factor = ROOT_THREE / length_ref[0]
    variance = variance_ref[0]
    regions = regions_ref[...]
    nugget = jnp.zeros((8, 128), F32)
    for g in range(NREG):
        nugget = jnp.where(regions == g, nugget_ref[g], nugget)
    obs[0] = jnp.concatenate(
        [bins_ref[...].astype(F32), fraction_ref[...], weights_ref[...], jnp.zeros((8, 104), F32)],
        axis=1,
    )
    pad = jnp.zeros((120, 128), F32)
    x_rows = jnp.transpose(jnp.concatenate([coords_ref[0], pad], axis=0)) * factor
    y_rows = jnp.transpose(jnp.concatenate([coords_ref[1], pad], axis=0)) * factor
    diagonal = iota((128, 128), 0) == iota((128, 128), 1)

    def pick_row(x):
        return jnp.sum(jnp.where(iota((8, 128), 0) == tile_at[0:8], x, 0.0), axis=0, keepdims=True)

    def pick(tiles, rows):
        found = tiles(0)
        for b in range(1, 8):
            found = jnp.where(tile_at[0:rows] == b, tiles(b), found)
        return found

    @pl.when(r == d)
    def _():
        pivot_info[...] = jnp.concatenate(
            [
                pick_row(coords_ref[0]),
                pick_row(coords_ref[1]),
                pick_row(nugget),
                jnp.zeros((5, 128), F32),
            ],
            axis=0,
        )

    load.wait()

    @pl.when(c == d)
    def _():
        def rows_of(i, carry):
            row_raw[pl.ds(pl.multiple_of(i * 32, 32), 32), :] = pick(
                lambda b: corr[pl.ds(i * 256 + b, 32, stride=8), :], 32
            )
            return carry

        lax.fori_loop(0, 32, rows_of, 0)

    @pl.when(r == d)
    def _():
        def cols_of(i, carry):
            at = pl.multiple_of(i * 32, 32)
            col_raw[pl.ds(at, 32), :] = pick(lambda b: corr[pl.ds(b * 1024 + at, 32), :], 32)
            return carry

        lax.fori_loop(0, 32, cols_of, 0)

    @pl.when((r == d) & (c == d))
    def _():
        info = pivot_info[...]
        across = jnp.transpose(info)
        px = info[0:1, :] * factor
        py = info[1:2, :] * factor
        tile = matern(across[:, 0:1] * factor - px, across[:, 1:2] * factor - py, variance)
        work[...] = tile + jnp.where(diagonal, info[2:3, :], 0.0)

        def own_tile(i, carry):
            at = pl.ds(pl.multiple_of(i * 32, 32), 32)
            work[at, :] = work[at, :] - pick(lambda b: row_raw[pl.ds(b * 128 + i * 32, 32), :], 32)
            return carry

        lax.fori_loop(0, 4, own_tile, 0)
        factor_inverse(work, inverse)
        factor_rx[8 * d : 8 * d + 8, :] = inverse[8 * d : 8 * d + 8, :]

    pl.semaphore_wait(barrier, 2 * (N - 1))

    @pl.when(r == d)
    def _():
        each_peer(lambda i: send_to(pivot_info, pivot_info, S_PIVOT, (row_peer(i), c)))

    @pl.when(r == c)
    def _():
        each_peer(lambda i: send_to(coords_ref, col_sites, S_SITES, (row_peer(i), c)))
        col_sites[...] = coords_ref[...]

    @pl.when((r == d) & (c == d))
    def _():
        each_peer(
            lambda i: send_to(
                rows8(inverse, col_peer(i)), rows8(factor_rx, col_peer(i)), S_F1, (r, col_peer(i))
            )
        )

    each_peer(lambda i: send_to(obs.at[0], obs.at[i], S_OBS, (r, col_peer(i))))

    @pl.when(r == d)
    def _():
        each_peer(
            lambda i: send_to(
                piece(col_raw, row_peer(i)), piece(col_raw, row_peer(i)), S_C1, (row_peer(i), c)
            )
        )

    @pl.when(c == d)
    def _():
        each_peer(
            lambda i: send_to(
                piece(row_raw, col_peer(i)), piece(row_raw, col_peer(i)), S_R1, (r, col_peer(i))
            )
        )

    @pl.when((r == d) & (c != d))
    def _():
        wait(rows8(factor_rx, c), recv.at[S_F1])

    @pl.when(r == d)
    def _():
        each_peer(
            lambda i: send_to(rows8(factor_rx, c), rows8(factor_rx, c), S_F2, (row_peer(i), c))
        )

    def share_row(i):
        to = col_peer(2 * i)

        @pl.when(to != d)
        def _():
            send_to(piece(row_raw, c), piece(row_raw, c), S_R2, (r, to), row_recv.at[c // 2])

    @pl.when(c != d)
    def _():
        wait(piece(row_raw, c), recv.at[S_R1])

    def share_row_step(i, carry):
        share_row(i)
        return carry

    lax.fori_loop(1, 8, share_row_step, 0)

    @pl.when(sibling != d)
    def _():
        send_to(piece(row_raw, c), piece(row_raw, c), S_R3, (r, sibling))

    @pl.when(r != d)
    def _():
        wait(piece(col_raw, r), recv.at[S_C1])

    def share_col(i):
        @pl.when(row_peer(i) != d)
        def _():
            send_to(piece(col_raw, r), piece(col_raw, r), S_C2, (row_peer(i), c))

    each_peer(share_col)

    wait(obs.at[pl.ds(1, 15)], recv.at[S_OBS])
    lane = iota((8, 128), 1)

    def unpack(i, found):
        source = lax.rem(c - i + N, N)
        packed = obs[i]
        here = (lane // 8) == source
        return tuple(
            jnp.where(here, pltpu.roll(packed, lax.rem(8 * source - 8 * j + 128, 128), 1), found[j])
            for j in range(3)
        )

    found = lax.fori_loop(0, N, unpack, tuple(jnp.zeros((8, 128), F32) for _ in range(3)))
    for j in range(3):
        sites[j] = found[j]

    @pl.when(r == d)
    def _():
        pivot_obs[...] = jnp.concatenate(
            [
                pick_row(found[0]),
                pick_row(found[1]),
                jnp.zeros((6, 128), F32),
            ],
            axis=0,
        )
        each_peer(lambda i: send_to(pivot_obs, pivot_obs, S_PO, (row_peer(i), c)))

    level = iota((128, 128), 0)

    def count(a, total):
        bins_i = sites[0, pl.ds(a, 1), :].astype(I32)
        high_i = (bins_i // 256) * 8 + (bins_i // 128) % 2
        weighted = jnp.where(level == high_i, sites[2, pl.ds(a, 1), :], 0.0)
        wh, wl = split2(weighted)
        low = (level == bins_i % 128).astype(F32).astype(BF16)
        return total + lax.dot_general(
            jnp.concatenate([wh, wl], axis=1),
            jnp.concatenate([low, low], axis=1),
            NT,
            preferred_element_type=F32,
        )

    hist[...] = lax.fori_loop(0, 8, count, jnp.zeros((128, 128), F32))
    each_peer(lambda i: send_to(rows8(hist, c), hist_rx.at[i], S_H2, (row_peer(i), c)))

    @pl.when(r != d)
    def _():
        wait(rows8(factor_rx, c), recv.at[S_F2])

    each_peer(lambda i: send_to(rows8(factor_rx, c), rows8(factor_rx, c), S_F3, (r, col_peer(i))))

    def pass_on(i):
        source = lax.rem(c + 16 - 2 * i, N)
        wait(piece(row_raw, source), row_recv.at[source // 2])

        @pl.when(sibling != d)
        def _():
            send_to(piece(row_raw, source), piece(row_raw, source), S_R3, (r, sibling))

    def pass_own(i):
        source = lax.rem(c + 16 - 2 * i, N)
        send_to(piece(row_raw, source), piece(row_raw, source), S_R3, (r, sibling))

    def pass_piece(i):
        @pl.when(c != d)
        def _():
            pass_on(i)

        @pl.when(c == d)
        def _():
            pass_own(i)

    @pl.when(r != c)
    def _():
        wait(col_sites, recv.at[S_SITES])

    col_x = col_sites[0] * factor
    col_y = col_sites[1] * factor
    place = iota((8, 128), 0) * 128 + lane
    own_nugget = jnp.where(r == c, nugget, 0.0)

    def form(a, carry_a):
        def eight(q, carry):
            for u in range(8):
                t = q * 8 + u
                at = pl.ds(pl.multiple_of(a * 1024 + t * 8, 8), 8)
                value = matern(
                    coords_s[0, a, t] * factor - col_x, coords_s[1, a, t] * factor - col_y, variance
                )
                value = value + jnp.where(place == a * 128 + t, own_nugget, 0.0)
                corr[at, :] = value - corr[at, :]
            return carry

        lax.fori_loop(0, 16, eight, 0)
        at = pl.ds(pl.multiple_of(a * 1024, 1024), 1024)
        pltpu.make_async_copy(corr.at[at], matrix_hbm.at[at], out_sem).start()


        @pl.when(a == 2)
        def _():
            wait(hist_rx.at[pl.ds(1, 15)], recv.at[S_H2])
            own = pl.ds(pl.multiple_of(c * 8, 8), 8)
            hist_all[own, :] = lax.fori_loop(
                1, N, lambda i, total: total + hist_rx[i], hist[own, :]
            )
            each_peer(
                lambda i: send_to(rows8(hist_all, c), rows8(hist_all, c), S_H3, (r, col_peer(i)))
            )

        @pl.when(a >= 1)
        def _():
            pass_piece(a)

        return carry_a

    lax.fori_loop(0, 8, form, 0)

    @pl.when(r != d)
    def _():
        wait(pivot_info, recv.at[S_PIVOT])

    info = pivot_info[...]
    across = jnp.transpose(info)
    px = info[0:1, :] * factor
    py = info[1:2, :] * factor
    pnug = jnp.where(diagonal, info[2:3, :], 0.0)
    tx = across[:, 0:1] * factor
    ty = across[:, 1:2] * factor

    def panels(a, carry):
        at = pl.ds(pl.multiple_of(a * 128, 128), 128)
        turn = lax.rem(128 - a, 128)
        x = pltpu.roll(x_rows, turn, 1)[:, 0:1]
        y = pltpu.roll(y_rows, turn, 1)[:, 0:1]
        extra = jnp.where(tile_at == a, pnug, 0.0)
        rows_out[at, :] = matern(x - px, y - py, variance) + jnp.where(r == d, extra, 0.0)
        x = col_sites[0, pl.ds(a, 1), :] * factor
        y = col_sites[1, pl.ds(a, 1), :] * factor
        cols_out[a] = matern(tx - x, ty - y, variance) + jnp.where(c == d, extra, 0.0)
        return carry

    lax.fori_loop(0, 8, panels, 0)

    @pl.when(r != d)
    def _():
        wait(col_raw.at[pl.ds(0, 15 * PIECE)], recv.at[S_C2])
        wait(pivot_obs, recv.at[S_PO])


    def less_cols(b, carry):
        cols_out[b] = cols_out[b] - col_raw[pl.ds(b, 128, stride=8), :]
        return carry

    lax.fori_loop(0, 8, less_cols, 0)
    sites_out[...] = sites[...]
    pivot_out[...] = pivot_obs[...]
    wait(factor_rx.at[pl.ds(0, 120)], recv.at[S_F3])
    inverse_out[...] = factor_rx[...]
    wait(hist_all.at[pl.ds(0, 120)], recv.at[S_H3])
    hist_out[...] = hist_all[...]

    @pl.when(c != d)
    def _():
        wait(row_raw.at[pl.ds(0, 8 * PIECE)], recv.at[S_R3])

    def less_rows(a, carry):
        at = pl.ds(pl.multiple_of(a * 128, 128), 128)
        rows_out[at, :] = rows_out[at, :] - row_raw[at, :]
        return carry

    lax.fori_loop(0, 8, less_rows, 0)

    def sent(ref, which):
        wait(ref, send.at[which])

    @pl.when(r == d)
    def _():
        sent(hist.at[pl.ds(0, 120)], S_PIVOT)
        sent(hist.at[pl.ds(0, 120)], S_F2)
        sent(hist.at[pl.ds(0, 120)], S_PO)
        sent(col_raw.at[pl.ds(0, 15 * PIECE)], S_C1)
        sent(col_raw.at[pl.ds(0, 15 * PIECE)], S_C2)

    @pl.when(r != d)
    def _():
        sent(col_raw.at[pl.ds(0, 14 * PIECE)], S_C2)

    @pl.when(r == c)
    def _():
        sent(row_raw.at[pl.ds(0, 240)], S_SITES)

    @pl.when((r == d) & (c == d))
    def _():
        sent(hist.at[pl.ds(0, 120)], S_F1)

    @pl.when(c == d)
    def _():
        sent(row_raw.at[pl.ds(0, 15 * PIECE)], S_R1)

    for which in (S_OBS, S_F3, S_H2, S_H3):
        sent(hist.at[pl.ds(0, 120)], which)

    same_place = lax.rem(c, 2) == d % 2

    @pl.when(same_place & (c != d))
    def _():
        sent(row_raw.at[pl.ds(0, 6 * PIECE)], S_R2)

    @pl.when(jnp.logical_not(same_place) | (c == d))
    def _():
        sent(row_raw.at[pl.ds(0, 7 * PIECE)], S_R2)

    @pl.when(sibling != d)
    def _():
        sent(row_raw.at[pl.ds(0, 8 * PIECE)], S_R3)

    wait(corr, out_sem)


def exchange(d, *args):
    vmem = pl.BlockSpec(memory_space=pltpu.VMEM)
    smem = pl.BlockSpec(memory_space=pltpu.SMEM)
    hbm = pl.BlockSpec(memory_space=pl.ANY)
    shape = lambda *s: jax.ShapeDtypeStruct(s, F32)
    return pl.pallas_call(
        functools.partial(exchange_kernel, d),
        out_shape=(
            shape(8192, 128),
            shape(1024, 128),
            shape(8, 128, 128),
            shape(128, 128),
            shape(128, 128),
            shape(3, 8, 128),
            shape(8, 128),
        ),
        in_specs=[smem] * 5 + [vmem] * 5 + [hbm],
        out_specs=(hbm,) + (vmem,) * 6,
        scratch_shapes=[
            pltpu.VMEM((8192, 128), F32),
            pltpu.VMEM((1024, 128), F32),
            pltpu.VMEM((1024, 128), F32),
            pltpu.VMEM((128, 128), F32),
            pltpu.VMEM((128, 128), F32),
            pltpu.VMEM((128, 128), F32),
            pltpu.VMEM((2, 8, 128), F32),
            pltpu.VMEM((8, 128), F32),
            pltpu.VMEM((N, 8, 128), F32),
            pltpu.VMEM((128, 128), F32),
            pltpu.VMEM((N, 8, 128), F32),
            pltpu.VMEM((128, 128), F32),
            pltpu.VMEM((3, 8, 128), F32),
            pltpu.VMEM((8, 128), F32),
            pltpu.SemaphoreType.DMA,
            pltpu.SemaphoreType.DMA,
            pltpu.SemaphoreType.DMA((14,)),
            pltpu.SemaphoreType.DMA((14,)),
            pltpu.SemaphoreType.DMA((8,)),
        ],
        compiler_params=pltpu.CompilerParams(
            collective_id=d, has_side_effects=True, vmem_limit_bytes=24 * MIB
        ),
        name="exchange",
    )(*args)


def quantile(x):
    w = -jnp.log((1.0 - x) * (1.0 + x)) - 2.5
    p = jnp.full_like(w, 2.81022636e-08)
    for coefficient in (
        3.43273939e-07,
        -3.5233877e-06,
        -4.39150654e-06,
        0.00021858087,
        -0.00125372503,
        -0.00417768164,
        0.246640727,
        1.50140941,
    ):
        p = coefficient + p * w
    return p * x


def update_kernel(
    k_ref,
    matrix_ref,
    rows_ref,
    cols_ref,
    inverse_ref,
    hist_ref,
    sites_ref,
    pivot_ref,
    trailing_ref,
    panel_ref,
    scores_ref,
    terms_ref,
    cols_panel,
    scores,
    solved,
):
    a = pl.program_id(0)
    inverse = inverse_ref[...]

    @pl.when(a == 0)
    def _():
        cols = jnp.concatenate([cols_ref[b] for b in range(8)], axis=1)
        panel = dot3(inverse, cols, NN)
        high, low = split2(panel)
        cols_panel[0:128, :] = high
        cols_panel[128:256, :] = low
        cols_panel[256:384, :] = high

        counts = hist_ref[...]
        level = iota((128, 128), 0)
        across = iota((128, 128), 1)
        parts = split3(counts)
        ahead = (across < level).astype(F32).astype(BF16)
        earlier = (level < across).astype(F32).astype(BF16)
        above = jnp.zeros((128, 128), F32)
        along = jnp.zeros((128, 128), F32)
        for part in parts:
            above = above + lax.dot_general(ahead, part, NN, preferred_element_type=F32)
            along = along + lax.dot_general(part, earlier, NN, preferred_element_type=F32)
        before = jnp.sum(above, axis=1, keepdims=True) + along
        total = jnp.sum(jnp.sum(counts, axis=1, keepdims=True), axis=0, keepdims=True)

        bins_f = jnp.concatenate([sites_ref[0], pivot_ref[...]], axis=0)
        fraction = jnp.concatenate([sites_ref[1], pivot_ref[...]], axis=0)
        bins_i = bins_f.astype(I32)
        high_i = (bins_i // 256) * 8 + (bins_i // 128) % 2
        low_i = bins_i % 128
        high_hot = jnp.concatenate(
            [(level == high_i[i : i + 1, :]).astype(F32).astype(BF16) for i in range(9)], axis=1
        )
        tripled = jnp.concatenate([high_hot] * 3, axis=0)
        look = [
            lax.dot_general(
                jnp.concatenate(split3(table), axis=0), tripled, TN, preferred_element_type=F32
            )
            for table in (before, counts)
        ]
        probs = []
        for i in range(9):
            hot = level == low_i[i : i + 1, :]
            at = slice(i * 128, (i + 1) * 128)
            start = jnp.sum(jnp.where(hot, look[0][:, at], 0.0), axis=0, keepdims=True)
            count = jnp.sum(jnp.where(hot, look[1][:, at], 0.0), axis=0, keepdims=True)
            part = fraction[i : i + 1, :] if i < 8 else fraction[9:10, :]
            probs.append((start + part * count) / total)
        probs = jnp.concatenate(probs + [jnp.full((7, 128), 0.5, F32)], axis=0)
        found = ROOT_TWO * quantile(2.0 * jnp.clip(probs, 0.01, 0.99) - 1.0)
        scores[...] = found[0:8, :]
        z = dot3(jnp.broadcast_to(found[8:9, :], (8, 128)), inverse, NT)
        solved[...] = z
        diagonal = jnp.sum(jnp.where(level == across, inverse, 0.0), axis=0, keepdims=True)
        terms_ref[0] = -2.0 * jnp.sum(jnp.log(diagonal))
        terms_ref[1] = jnp.sum(z[0:1, :] * z[0:1, :])

    panel = dot3(rows_ref[...], inverse, NT)
    panel_ref[...] = panel
    high, low = split2(panel)
    update = lax.dot_general(
        jnp.concatenate([high, high, low], axis=1), cols_panel[...], NN, preferred_element_type=F32
    )
    for b in range(8):
        at = pl.ds(b, 128, stride=8)
        trailing_ref[at, :] = matrix_ref[at, :] - update[:, b * 128 : (b + 1) * 128]
    z = solved[...]
    moved = scores[pl.ds(a, 1), :] - dot3(z, panel, NT)[0:1, :]
    k = k_ref[0]
    is_pivot = (lax.axis_index("row") == k % N) & (a == k // N)
    scores_ref[pl.ds(a, 1), :] = jnp.where(is_pivot, z[0:1, :], moved)


def update(k, matrix, rows, cols, inverse, hist, sites, pivot):
    shape = lambda *s: jax.ShapeDtypeStruct(s, F32)
    whole = lambda *s: pl.BlockSpec(s, lambda a: (0,) * len(s))
    smem = pl.BlockSpec(memory_space=pltpu.SMEM)
    return pl.pallas_call(
        update_kernel,
        grid=(8,),
        out_shape=(shape(8192, 128), shape(1024, 128), shape(8, 128), shape(2)),
        in_specs=[
            smem,
            pl.BlockSpec((1024, 128), lambda a: (a, 0)),
            pl.BlockSpec((128, 128), lambda a: (a, 0)),
            whole(8, 128, 128),
            whole(128, 128),
            whole(128, 128),
            whole(3, 8, 128),
            whole(8, 128),
        ],
        out_specs=(
            pl.BlockSpec((1024, 128), lambda a: (a, 0)),
            pl.BlockSpec((128, 128), lambda a: (a, 0)),
            whole(8, 128),
            smem,
        ),
        scratch_shapes=[
            pltpu.VMEM((384, 1024), BF16),
            pltpu.VMEM((8, 128), F32),
            pltpu.VMEM((8, 128), F32),
        ],
        compiler_params=pltpu.CompilerParams(vmem_limit_bytes=24 * MIB),
        name="update",
    )(k, matrix, rows, cols, inverse, hist, sites, pivot)


def on_device(
    panel_index,
    coords,
    region_ids,
    nugget,
    variance,
    length,
    correction,
    bin_index,
    fraction,
    weights,
):
    coords = coords.reshape(2, 8, 128)
    args = (
        panel_index,
        nugget,
        variance,
        length,
        coords,
        coords,
        region_ids.reshape(8, 128),
        bin_index.reshape(8, 8),
        fraction.reshape(8, 8),
        weights.reshape(8, 8),
        correction.reshape(8192, 128),
    )
    branches = [functools.partial(exchange, d) for d in range(N)]
    moved = lax.switch(panel_index[0] % N, branches, *args)
    trailing, panel, scores, terms = update(panel_index, *moved)
    return (
        trailing.reshape(8, 1, 128, 8, 1, 128),
        panel.reshape(8, 1, 128, 128),
        scores.reshape(8, 1, 128),
        terms,
    )


def solution(mesh):
    in_specs = (
        P(),
        P(None, None, "row", None),
        P(None, "row", None),
        P(),
        P(),
        P(),
        P(None, "row", None, None, "col", None),
        P(None, "row", "col", None),
        P(None, "row", "col", None),
        P(None, "row", "col", None),
    )
    out_specs = (
        P(None, "row", None, None, "col", None),
        P(None, "row", None, None),
        P(None, "row", None),
        P(),
    )
    return jax.shard_map(
        on_device, mesh=mesh, in_specs=in_specs, out_specs=out_specs, check_vma=False
    )
```

```python
import functools

import jax
import jax.numpy as jnp
from jax import lax
from jax.experimental import pallas as pl
from jax.experimental.pallas import tpu as pltpu
from jax.sharding import PartitionSpec as P

F32 = jnp.float32
BF16 = jnp.bfloat16
I32 = jnp.int32
MESH = pl.DeviceIdType.MESH
N = 16
NREG = 16
ROOT_THREE = 1.7320508075688772
ROOT_TWO = 1.4142135623730951
NT = (((1,), (1,)), ((), ()))
NN = (((1,), (0,)), ((), ()))
TN = (((0,), (0,)), ((), ()))
PIECE = 64
EARLY = 2
KEPT = 4
MIB = 2**20


def iota(shape, dim):
    return lax.broadcasted_iota(I32, shape, dim)


def split2(x):
    high = x.astype(BF16)
    return high, (x - high.astype(F32)).astype(BF16)


def split3(x):
    high = x.astype(BF16)
    rest = x - high.astype(F32)
    mid = rest.astype(BF16)
    return high, mid, (rest - mid.astype(F32)).astype(BF16)


def dot3(a, b, dims):
    (ca,), (cb,) = dims[0]
    ah, al = split2(a)
    bh, bl = split2(b)
    return lax.dot_general(
        jnp.concatenate([ah, ah, al], axis=ca),
        jnp.concatenate([bh, bl, bh], axis=cb),
        dims,
        preferred_element_type=F32,
    )


def matern(dx, dy, variance):
    scaled = jnp.sqrt(dx * dx + dy * dy)
    return (variance + variance * scaled) * jnp.exp(-scaled)


def factor_inverse(work, inv):
    nb = 16
    groups = nb // 8
    sub = iota((8, 128), 0)
    lane = iota((nb, 128), 1)
    inv[...] = (iota((128, 128), 0) == iota((128, 128), 1)).astype(F32)

    def block(p, carry):
        rows_k = [work[8 * g : 8 * g + 8, :] for g in range(groups)]
        rows_i = [inv[8 * g : 8 * g + 8, :] for g in range(groups)]
        col = [
            [
                jnp.broadcast_to(rows_k[g][:, q : q + 1], (8, 128)) if 8 * g + 7 >= q else None
                for g in range(groups)
            ]
            for q in range(nb)
        ]
        pivots = [jnp.ones((8, 128), F32) for _ in range(groups)]
        for j in range(nb):
            gj, sj = divmod(j, 8)
            pivot = jnp.broadcast_to(col[j][gj][sj : sj + 1, :], (8, 128))
            pivots[gj] = jnp.where(sub == sj, pivot, pivots[gj])
            if j == nb - 1:
                break
            recip = 1.0 / pivot
            mult = [None] * groups
            for g in range(gj, groups):
                m = col[j][g] * recip
                mult[g] = jnp.where(sub > sj, m, 0.0) if g == gj else m
            for q in range(j + 1, nb):
                gq, sq = divmod(q, 8)
                scale = jnp.broadcast_to(col[j][gq][sq : sq + 1, :], (8, 128))
                for g in range(gq, groups):
                    col[q][g] = col[q][g] - mult[g] * scale
            row_k = jnp.broadcast_to(rows_k[gj][sj : sj + 1, :], (8, 128))
            row_i = jnp.broadcast_to(rows_i[gj][sj : sj + 1, :], (8, 128))
            for g in range(gj, groups):
                if 8 * g + 7 > j:
                    rows_k[g] = rows_k[g] - mult[g] * row_k
                    rows_i[g] = rows_i[g] - mult[g] * row_i
        roots = [lax.rsqrt(x) for x in pivots]
        upper = jnp.concatenate([rows_k[g] * roots[g] for g in range(groups)], axis=0)
        done = jnp.concatenate([rows_i[g] * roots[g] for g in range(groups)], axis=0)
        below = jnp.where((lane >= nb) & (lane < 128 - nb * p), upper, 0.0)
        h, m, l = split3(below)
        h2, m2, l2 = split3(done)
        left = jnp.concatenate([h, h, m, m, h, l], axis=0)
        right = jnp.concatenate(
            [
                jnp.concatenate([h, m, h, m, l, h], axis=0),
                jnp.concatenate([h2, m2, h2, m2, l2, h2], axis=0),
            ],
            axis=1,
        )
        update = lax.dot_general(left, right, TN, preferred_element_type=F32)
        next_k = work[nb:, :] - update[nb:, :128]
        next_i = inv[nb:, :] - update[nb:, 128:]
        work[0 : 128 - nb, :] = pltpu.roll(next_k, 128 - nb, 1)
        inv[0 : 128 - nb, :] = next_i
        inv[128 - nb :, :] = done
        return carry

    lax.fori_loop(0, 128 // nb, block, 0)


def exchange_kernel(
    d,
    k_hbm,
    nugget_hbm,
    variance_hbm,
    length_hbm,
    coords_hbm,
    regions_hbm,
    bins_hbm,
    fraction_hbm,
    weights_hbm,
    corr_hbm,
    *refs,
):
    matrix_out = refs[:8]
    exchange_body(
        d,
        (
            k_hbm,
            nugget_hbm,
            variance_hbm,
            length_hbm,
            coords_hbm,
            regions_hbm,
            bins_hbm,
            fraction_hbm,
            weights_hbm,
        ),
        corr_hbm,
        matrix_out,
        *refs[8:],
    )


def exchange_body(
    d,
    small_hbm,
    corr_hbm,
    matrix_out,
    rows_out,
    cols_out,
    inverse_out,
    hist_out,
    sites_out,
    pivot_out,
    k_ref,
    nugget_ref,
    variance_ref,
    length_ref,
    coords_s,
    coords_ref,
    regions_ref,
    bins_ref,
    fraction_ref,
    weights_ref,
    corr,
    row_raw,
    col_raw,
    work,
    inverse,
    factor_rx,
    col_sites,
    pivot_info,
    hist,
    hist_rx,
    hist_sum,
    hist_rx2,
    hist_all,
    pivot_obs,
    in_sem,
    small_sem,
    out_sem,
    send,
    recv,
    row_recv,
):
    (
        k_hbm,
        nugget_hbm,
        variance_hbm,
        length_hbm,
        coords_hbm,
        regions_hbm,
        bins_hbm,
        fraction_hbm,
        weights_hbm,
    ) = small_hbm
    r = lax.axis_index("row")
    c = lax.axis_index("col")
    sibling = c + 1 - 2 * lax.rem(c, 2)
    (
        S_SITES, S_PIVOT, S_OBS, S_F1, S_F2, S_F3, S_H2, S_H3, S_PO, S_R1, S_R2, S_R3, S_C1, S_C2, S_H1,
    ) = range(15)

    def row_peer(i):
        return lax.rem(r + i, N)

    def col_peer(i):
        return lax.rem(c + i, N)

    def send_to(src, dst, which, to, sem=None):
        pltpu.make_async_remote_copy(
            src_ref=src,
            dst_ref=dst,
            send_sem=send.at[which],
            recv_sem=recv.at[which] if sem is None else sem,
            device_id=to,
            device_id_type=MESH,
        ).start()

    def wait(ref, sem):
        pltpu.make_async_copy(ref, ref, sem).wait()

    def each_peer(body):
        def step(i, carry):
            body(i)
            return carry

        lax.fori_loop(1, N, step, 0)

    def rows8(ref, i):
        return ref.at[pl.ds(pl.multiple_of(i * 8, 8), 8)]

    def piece(ref, i):
        return ref.at[pl.ds(pl.multiple_of(i * PIECE, PIECE), PIECE)]

    barrier = pltpu.get_barrier_semaphore()

    def greet(i):
        pl.semaphore_signal(barrier, inc=1, device_id=(row_peer(i), c), device_id_type=MESH)
        pl.semaphore_signal(barrier, inc=1, device_id=(r, col_peer(i)), device_id_type=MESH)

    each_peer(greet)
    load = pltpu.make_async_copy(corr_hbm, corr, in_sem)
    small = [
        pltpu.make_async_copy(src, dst, small_sem.at[i])
        for i, (src, dst) in enumerate(
            (
                (coords_hbm, coords_s),
                (coords_hbm, coords_ref),
                (regions_hbm, regions_ref),
                (bins_hbm, bins_ref),
                (fraction_hbm, fraction_ref),
                (weights_hbm, weights_ref),
                (k_hbm, k_ref),
                (nugget_hbm, nugget_ref),
                (variance_hbm, variance_ref),
                (length_hbm, length_ref),
            )
        )
    ]
    for copy in small:
        copy.start()
    load.start()
    for copy in small:
        copy.wait()

    tile_at = jnp.full((128, 128), k_ref[0] // N, I32)
    factor = ROOT_THREE / length_ref[0]
    variance = variance_ref[0]
    regions = regions_ref[...]
    nugget = jnp.zeros((8, 128), F32)
    for g in range(NREG):
        nugget = jnp.where(regions == g, nugget_ref[g], nugget)
    obs = jnp.concatenate(
        [bins_ref[...].astype(F32), fraction_ref[...], weights_ref[...], jnp.zeros((8, 104), F32)],
        axis=1,
    )
    lane = iota((8, 128), 1)
    level = iota((128, 128), 0)

    def one_row(x):
        spread = pltpu.roll(x, 0, 1, stride=8, stride_axis=0)
        return jnp.sum(jnp.where(lane // 8 == iota((8, 128), 0), spread, 0.0), axis=0, keepdims=True)

    own_bins_f = one_row(obs)
    own_fraction = one_row(pltpu.roll(obs, 128 - 8, 1))
    own_weights = one_row(pltpu.roll(obs, 128 - 16, 1))
    own_bins = own_bins_f.astype(I32)
    weighted = jnp.where(level == (own_bins // 256) * 8 + (own_bins // 128) % 2, own_weights, 0.0)
    wh, wl = split2(weighted)
    low = (level == own_bins % 128).astype(F32).astype(BF16)
    counts = lax.dot_general(
        jnp.concatenate([wh, wl], axis=1),
        jnp.concatenate([low, low], axis=1),
        NT,
        preferred_element_type=F32,
    )
    own_row = jnp.where(lane[0:1] < 64, own_bins_f, pltpu.roll(jnp.broadcast_to(own_fraction, (8, 128)), 64, 1)[0:1])
    hist[...] = jnp.where(level % 8 == 2, own_row, counts)

    pad = jnp.zeros((120, 128), F32)
    x_rows = jnp.transpose(jnp.concatenate([coords_ref[0], pad], axis=0)) * factor
    y_rows = jnp.transpose(jnp.concatenate([coords_ref[1], pad], axis=0)) * factor
    diagonal = iota((128, 128), 0) == iota((128, 128), 1)

    def pick_row(x):
        return jnp.sum(jnp.where(iota((8, 128), 0) == tile_at[0:8], x, 0.0), axis=0, keepdims=True)

    def pick(tiles, rows):
        found = tiles(0)
        for b in range(1, 8):
            found = jnp.where(tile_at[0:rows] == b, tiles(b), found)
        return found

    @pl.when(r == d)
    def _():
        pivot_info[...] = jnp.concatenate(
            [
                pick_row(coords_ref[0]),
                pick_row(coords_ref[1]),
                pick_row(nugget),
                jnp.zeros((5, 128), F32),
            ],
            axis=0,
        )

    load.wait()

    @pl.when(c == d)
    def _():
        def rows_of(i, carry):
            row_raw[pl.ds(pl.multiple_of(i * 32, 32), 32), :] = pick(
                lambda b: corr[pl.ds(i * 256 + b, 32, stride=8), :], 32
            )
            return carry

        lax.fori_loop(0, 32, rows_of, 0)

    @pl.when(r == d)
    def _():
        def cols_of(i, carry):
            at = pl.multiple_of(i * 32, 32)
            col_raw[pl.ds(at, 32), :] = pick(lambda b: corr[pl.ds(b * 1024 + at, 32), :], 32)
            return carry

        lax.fori_loop(0, 32, cols_of, 0)

    @pl.when((r == d) & (c == d))
    def _():
        info = pivot_info[...]
        across = jnp.transpose(info)
        px = info[0:1, :] * factor
        py = info[1:2, :] * factor
        tile = matern(across[:, 0:1] * factor - px, across[:, 1:2] * factor - py, variance)
        work[...] = tile + jnp.where(diagonal, info[2:3, :], 0.0)

        def own_tile(i, carry):
            at = pl.ds(pl.multiple_of(i * 32, 32), 32)
            work[at, :] = work[at, :] - pick(lambda b: row_raw[pl.ds(b * 128 + i * 32, 32), :], 32)
            return carry

        lax.fori_loop(0, 4, own_tile, 0)
        factor_inverse(work, inverse)
        factor_rx[8 * d : 8 * d + 8, :] = inverse[8 * d : 8 * d + 8, :]

    pl.semaphore_wait(barrier, 2 * (N - 1))

    @pl.when((r == d) & (c == d))
    def _():
        each_peer(
            lambda i: send_to(
                rows8(inverse, col_peer(i)), rows8(factor_rx, col_peer(i)), S_F1, (r, col_peer(i))
            )
        )

    @pl.when(r == d)
    def _():
        each_peer(
            lambda i: send_to(
                piece(col_raw, row_peer(i)), piece(col_raw, row_peer(i)), S_C1, (row_peer(i), c)
            )
        )

    each_peer(lambda i: send_to(rows8(hist, col_peer(i)), hist_rx.at[i], S_H1, (r, col_peer(i))))

    @pl.when(c == d)
    def _():
        each_peer(
            lambda i: send_to(
                piece(row_raw, col_peer(i)), piece(row_raw, col_peer(i)), S_R1, (r, col_peer(i))
            )
        )

    @pl.when(r == c)
    def _():
        each_peer(lambda i: send_to(coords_ref, col_sites, S_SITES, (row_peer(i), c)))
        col_sites[...] = coords_ref[...]

    @pl.when(r == d)
    def _():
        each_peer(lambda i: send_to(pivot_info, pivot_info, S_PIVOT, (row_peer(i), c)))

    @pl.when((r == d) & (c != d))
    def _():
        wait(rows8(factor_rx, c), recv.at[S_F1])

    @pl.when(r == d)
    def _():
        each_peer(
            lambda i: send_to(rows8(factor_rx, c), rows8(factor_rx, c), S_F2, (row_peer(i), c))
        )

    def share_row(i, carry):
        to = col_peer(2 * i)

        @pl.when(to != d)
        def _():
            send_to(piece(row_raw, c), piece(row_raw, c), S_R2, (r, to), row_recv.at[c // 2])

        return carry

    @pl.when(c != d)
    def _():
        wait(piece(row_raw, c), recv.at[S_R1])

    lax.fori_loop(1, 8, share_row, 0)

    @pl.when(sibling != d)
    def _():
        send_to(piece(row_raw, c), piece(row_raw, c), S_R3, (r, sibling))

    wait(hist_rx.at[pl.ds(1, 15)], recv.at[S_H1])
    own = pl.ds(pl.multiple_of(c * 8, 8), 8)
    summed = lax.fori_loop(1, N, lambda i, total: total + hist_rx[i], hist[own, :])
    hist_sum[...] = jnp.where(iota((8, 128), 0) < 2, summed, 0.0)
    each_peer(lambda i: send_to(hist_sum, hist_rx2.at[i], S_H2, (row_peer(i), c)))

    @pl.when(r != c)
    def _():
        wait(col_sites, recv.at[S_SITES])

    col_x = col_sites[0] * factor
    col_y = col_sites[1] * factor
    place = iota((8, 128), 0) * 128 + lane
    own_nugget = jnp.where(r == c, nugget, 0.0)

    def form(a):
        def eight(q, carry):
            for u in range(8):
                t = q * 8 + u
                at = pl.ds(pl.multiple_of(a * 1024 + t * 8, 8), 8)
                value = matern(
                    coords_s[0, a, t] * factor - col_x, coords_s[1, a, t] * factor - col_y, variance
                )
                value = value + jnp.where(place == a * 128 + t, own_nugget, 0.0)
                corr[at, :] = value - corr[at, :]
            return carry

        lax.fori_loop(0, 16, eight, 0)
        for b in range(8):

            @pl.when(a == b)
            def _():
                at = pl.ds(b * 1024, 1024)
                pltpu.make_async_copy(corr.at[at], matrix_out[b], out_sem).start()

    lax.fori_loop(0, EARLY, lambda a, carry: (form(a), carry)[1], 0)

    @pl.when(r != d)
    def _():
        wait(piece(col_raw, r), recv.at[S_C1])

    def share_col(i):
        @pl.when(row_peer(i) != d)
        def _():
            send_to(piece(col_raw, r), piece(col_raw, r), S_C2, (row_peer(i), c))

    each_peer(share_col)

    @pl.when(r != d)
    def _():
        wait(rows8(factor_rx, c), recv.at[S_F2])

    each_peer(lambda i: send_to(rows8(factor_rx, c), rows8(factor_rx, c), S_F3, (r, col_peer(i))))

    hist_rx[0] = hist[own, :]

    def unpack(i, found):
        source = lax.rem(c - i + N, N)
        packed = jnp.broadcast_to(hist_rx[i][2:3, :], (8, 128))
        spread = pltpu.roll(packed, 0, 1, stride=8, stride_axis=0)
        here = (lane // 8) == source
        return tuple(
            jnp.where(
                here,
                pltpu.roll(spread, lax.rem(8 * source + 64 * j + 72, 128), 1),
                found[j],
            )
            for j in range(2)
        )

    found = lax.fori_loop(0, N, unpack, (jnp.zeros((8, 128), F32), jnp.zeros((8, 128), F32)))
    found = [jnp.concatenate([x[7 - a : 8 - a] for a in range(8)], axis=0) for x in found]
    for j in range(2):
        sites_out[j] = found[j]

    @pl.when(r == d)
    def _():
        pivot_obs[...] = jnp.concatenate(
            [pick_row(found[0]), pick_row(found[1]), jnp.zeros((6, 128), F32)], axis=0
        )
        each_peer(lambda i: send_to(pivot_obs, pivot_obs, S_PO, (row_peer(i), c)))

    def pass_on(i):
        source = lax.rem(c + 16 - 2 * i, N)
        wait(piece(row_raw, source), row_recv.at[source // 2])

        @pl.when(sibling != d)
        def _():
            send_to(piece(row_raw, source), piece(row_raw, source), S_R3, (r, sibling))

    def pass_own(i):
        source = lax.rem(c + 16 - 2 * i, N)
        send_to(piece(row_raw, source), piece(row_raw, source), S_R3, (r, sibling))

    def pass_piece(i):
        @pl.when(c != d)
        def _():
            pass_on(i)

        @pl.when(c == d)
        def _():
            pass_own(i)

    def later(a, carry):
        form(a)

        @pl.when(a == EARLY)
        def _():
            wait(hist_rx2.at[pl.ds(1, 15)], recv.at[S_H2])
            hist_all[own, :] = lax.fori_loop(
                1, N, lambda i, total: total + hist_rx2[i], hist_sum[...]
            )
            each_peer(
                lambda i: send_to(rows8(hist_all, c), rows8(hist_all, c), S_H3, (r, col_peer(i)))
            )

        pass_piece(a - 1)

        return carry

    lax.fori_loop(EARLY, 8, later, 0)
    lax.fori_loop(7, 8, lambda i, carry: (pass_piece(i), carry)[1], 0)

    @pl.when(r != d)
    def _():
        wait(pivot_info, recv.at[S_PIVOT])

    info = pivot_info[...]
    across = jnp.transpose(info)
    px = info[0:1, :] * factor
    py = info[1:2, :] * factor
    pnug = jnp.where(diagonal, info[2:3, :], 0.0)
    tx = across[:, 0:1] * factor
    ty = across[:, 1:2] * factor

    def panels(a, carry):
        at = pl.ds(pl.multiple_of(a * 128, 128), 128)
        turn = lax.rem(128 - a, 128)
        x = pltpu.roll(x_rows, turn, 1)[:, 0:1]
        y = pltpu.roll(y_rows, turn, 1)[:, 0:1]
        extra = jnp.where(tile_at == a, pnug, 0.0)
        rows_out[at, :] = matern(x - px, y - py, variance) + jnp.where(r == d, extra, 0.0)
        x = col_sites[0, pl.ds(a, 1), :] * factor
        y = col_sites[1, pl.ds(a, 1), :] * factor
        cols_out[a] = matern(tx - x, ty - y, variance) + jnp.where(c == d, extra, 0.0)
        return carry

    lax.fori_loop(0, 8, panels, 0)

    @pl.when(r != d)
    def _():
        wait(col_raw.at[pl.ds(0, 15 * PIECE)], recv.at[S_C2])
        wait(pivot_obs, recv.at[S_PO])


    def less_cols(b, carry):
        cols_out[b] = cols_out[b] - col_raw[pl.ds(b, 128, stride=8), :]
        return carry

    lax.fori_loop(0, 8, less_cols, 0)
    pivot_out[...] = pivot_obs[...]
    wait(factor_rx.at[pl.ds(0, 120)], recv.at[S_F3])
    inverse_out[...] = factor_rx[...]
    wait(hist_all.at[pl.ds(0, 120)], recv.at[S_H3])
    hist_out[...] = hist_all[...]

    @pl.when(c != d)
    def _():
        wait(row_raw.at[pl.ds(0, 8 * PIECE)], recv.at[S_R3])

    def less_rows(a, carry):
        at = pl.ds(pl.multiple_of(a * 128, 128), 128)
        rows_out[at, :] = rows_out[at, :] - row_raw[at, :]
        return carry

    lax.fori_loop(0, 8, less_rows, 0)

    def sent(ref, which):
        wait(ref, send.at[which])

    @pl.when(r == d)
    def _():
        sent(hist.at[pl.ds(0, 120)], S_PIVOT)
        sent(hist.at[pl.ds(0, 120)], S_F2)
        sent(hist.at[pl.ds(0, 120)], S_PO)
        sent(col_raw.at[pl.ds(0, 15 * PIECE)], S_C1)
        sent(col_raw.at[pl.ds(0, 15 * PIECE)], S_C2)

    @pl.when(r != d)
    def _():
        sent(col_raw.at[pl.ds(0, 14 * PIECE)], S_C2)

    @pl.when(r == c)
    def _():
        sent(row_raw.at[pl.ds(0, 240)], S_SITES)

    @pl.when((r == d) & (c == d))
    def _():
        sent(hist.at[pl.ds(0, 120)], S_F1)

    @pl.when(c == d)
    def _():
        sent(row_raw.at[pl.ds(0, 15 * PIECE)], S_R1)

    for which in (S_F3, S_H1, S_H2, S_H3):
        sent(hist.at[pl.ds(0, 120)], which)

    same_place = lax.rem(c, 2) == d % 2

    @pl.when(same_place & (c != d))
    def _():
        sent(row_raw.at[pl.ds(0, 6 * PIECE)], S_R2)

    @pl.when(jnp.logical_not(same_place) | (c == d))
    def _():
        sent(row_raw.at[pl.ds(0, 7 * PIECE)], S_R2)

    @pl.when(sibling != d)
    def _():
        sent(row_raw.at[pl.ds(0, 8 * PIECE)], S_R3)

    wait(corr, out_sem)


def exchange(d, *args):
    vmem = pl.BlockSpec(memory_space=pltpu.VMEM)
    hbm = pl.BlockSpec(memory_space=pl.ANY)
    far = pl.BlockSpec(memory_space=pltpu.HBM)
    shape = lambda *s: jax.ShapeDtypeStruct(s, F32)
    return pl.pallas_call(
        functools.partial(exchange_kernel, d),
        out_shape=(
            *[shape(1024, 128) for _ in range(KEPT)],
            *[pltpu.HBM((1024, 128), F32) for _ in range(8 - KEPT)],
            shape(1024, 128),
            shape(8, 128, 128),
            shape(128, 128),
            shape(128, 128),
            shape(2, 8, 128),
            shape(8, 128),
        ),
        in_specs=[hbm] * 10,
        out_specs=(vmem,) * KEPT + (far,) * (8 - KEPT) + (vmem,) * 6,
        scratch_shapes=[
            pltpu.SMEM((1,), I32),
            pltpu.SMEM((NREG,), F32),
            pltpu.SMEM((1,), F32),
            pltpu.SMEM((1,), F32),
            pltpu.SMEM((2, 8, 128), F32),
            pltpu.VMEM((2, 8, 128), F32),
            pltpu.VMEM((8, 128), I32),
            pltpu.VMEM((8, 8), I32),
            pltpu.VMEM((8, 8), F32),
            pltpu.VMEM((8, 8), F32),
            pltpu.VMEM((8192, 128), F32),
            pltpu.VMEM((1024, 128), F32),
            pltpu.VMEM((1024, 128), F32),
            pltpu.VMEM((128, 128), F32),
            pltpu.VMEM((128, 128), F32),
            pltpu.VMEM((128, 128), F32),
            pltpu.VMEM((2, 8, 128), F32),
            pltpu.VMEM((8, 128), F32),
            pltpu.VMEM((128, 128), F32),
            pltpu.VMEM((N, 8, 128), F32),
            pltpu.VMEM((8, 128), F32),
            pltpu.VMEM((N, 8, 128), F32),
            pltpu.VMEM((128, 128), F32),
            pltpu.VMEM((8, 128), F32),
            pltpu.SemaphoreType.DMA,
            pltpu.SemaphoreType.DMA((10,)),
            pltpu.SemaphoreType.DMA,
            pltpu.SemaphoreType.DMA((15,)),
            pltpu.SemaphoreType.DMA((15,)),
            pltpu.SemaphoreType.DMA((8,)),
        ],
        compiler_params=pltpu.CompilerParams(
            collective_id=d, has_side_effects=True, vmem_limit_bytes=12 * MIB
        ),
        name="exchange",
    )(*args)


def quantile(x):
    w = -jnp.log((1.0 - x) * (1.0 + x)) - 2.5
    p = jnp.full_like(w, 2.81022636e-08)
    for coefficient in (
        3.43273939e-07,
        -3.5233877e-06,
        -4.39150654e-06,
        0.00021858087,
        -0.00125372503,
        -0.00417768164,
        0.246640727,
        1.50140941,
    ):
        p = coefficient + p * w
    return p * x


def update_kernel(k_ref, *refs):
    matrix_ref = refs[:8]
    rows_ref, cols_ref, inverse_ref, hist_ref, sites_ref, pivot_ref = refs[8:14]
    trailing_hbm, panel_hbm, scores_ref, terms_ref = refs[14:18]
    trailing, panel, late, in_sem, out_sem, panel_sem = refs[18:]
    loads = [
        pltpu.make_async_copy(matrix_ref[a], late.at[a - KEPT], in_sem.at[a - KEPT])
        for a in range(KEPT, 8)
    ]
    for load in loads:
        load.start()
    inverse = inverse_ref[...]
    cols = dot3(inverse, jnp.concatenate([cols_ref[b] for b in range(8)], axis=1), NN)
    high, low = split2(cols)
    right = jnp.concatenate([high, low, high], axis=0)
    whole = dot3(rows_ref[...], inverse, NT)
    panel[...] = whole
    whole_high, whole_low = split2(whole)
    left = jnp.concatenate([whole_high, whole_high, whole_low], axis=1)

    counts = hist_ref[...]
    level = iota((128, 128), 0)
    across = iota((128, 128), 1)
    parts = split3(counts)
    ahead = (across < level).astype(F32).astype(BF16)
    earlier = (level < across).astype(F32).astype(BF16)
    above = jnp.zeros((128, 128), F32)
    along = jnp.zeros((128, 128), F32)
    for part in parts:
        above = above + lax.dot_general(ahead, part, NN, preferred_element_type=F32)
        along = along + lax.dot_general(part, earlier, NN, preferred_element_type=F32)
    before = jnp.sum(above, axis=1, keepdims=True) + along
    total = jnp.sum(jnp.sum(counts, axis=1, keepdims=True), axis=0, keepdims=True)

    bins_f = jnp.concatenate([sites_ref[0], pivot_ref[...]], axis=0)
    fraction = jnp.concatenate([sites_ref[1], pivot_ref[...]], axis=0)
    bins_i = bins_f.astype(I32)
    high_i = (bins_i // 256) * 8 + (bins_i // 128) % 2
    low_i = bins_i % 128
    high_hot = jnp.concatenate(
        [(level == high_i[i : i + 1, :]).astype(F32).astype(BF16) for i in range(9)], axis=1
    )
    tripled = jnp.concatenate([high_hot] * 3, axis=0)
    look = [
        lax.dot_general(
            jnp.concatenate(split3(table), axis=0), tripled, TN, preferred_element_type=F32
        )
        for table in (before, counts)
    ]
    probs = []
    for i in range(9):
        hot = level == low_i[i : i + 1, :]
        at = slice(i * 128, (i + 1) * 128)
        start = jnp.sum(jnp.where(hot, look[0][:, at], 0.0), axis=0, keepdims=True)
        count = jnp.sum(jnp.where(hot, look[1][:, at], 0.0), axis=0, keepdims=True)
        part = fraction[i : i + 1, :] if i < 8 else fraction[9:10, :]
        probs.append((start + part * count) / total)
    probs = jnp.concatenate(probs + [jnp.full((7, 128), 0.5, F32)], axis=0)
    found = ROOT_TWO * quantile(2.0 * jnp.clip(probs, 0.01, 0.99) - 1.0)
    z = dot3(jnp.broadcast_to(found[8:9, :], (8, 128)), inverse, NT)
    diagonal = jnp.sum(jnp.where(level == across, inverse, 0.0), axis=0, keepdims=True)
    terms_ref[0] = -2.0 * jnp.sum(jnp.log(diagonal))
    terms_ref[1] = jnp.sum(z[0:1, :] * z[0:1, :])
    moved = dot3(z, whole, NT)
    k = k_ref[0]
    here = lax.axis_index("row") == k % N
    for a in range(8):
        score = found[a : a + 1, :] - moved[0:1, a * 128 : (a + 1) * 128]
        scores_ref[a : a + 1, :] = jnp.where(here & (k // N == a), z[0:1, :], score)

    panel_copy = pltpu.make_async_copy(panel, panel_hbm, panel_sem)
    panel_copy.start()
    for a in range(8):
        change = lax.dot_general(
            left[a * 128 : (a + 1) * 128], right, NN, preferred_element_type=F32
        )
        block = matrix_ref[a] if a < KEPT else late.at[a - KEPT]
        if a >= KEPT:
            loads[a - KEPT].wait()
        for b in range(8):
            at = pl.ds(a * 1024 + b, 128, stride=8)
            before = block[pl.ds(b, 128, stride=8), :]
            trailing[at, :] = before - change[:, b * 128 : (b + 1) * 128]
        at = pl.ds(a * 1024, 1024)
        pltpu.make_async_copy(trailing.at[at], trailing_hbm.at[at], out_sem.at[a]).start()

    panel_copy.wait()
    for a in range(8):
        at = pl.ds(a * 1024, 1024)
        pltpu.make_async_copy(trailing.at[at], trailing_hbm.at[at], out_sem.at[a]).wait()


def update(*args):
    shape = lambda *s: jax.ShapeDtypeStruct(s, F32)
    vmem = pl.BlockSpec(memory_space=pltpu.VMEM)
    smem = pl.BlockSpec(memory_space=pltpu.SMEM)
    hbm = pl.BlockSpec(memory_space=pl.ANY)
    far = pl.BlockSpec(memory_space=pltpu.HBM)
    return pl.pallas_call(
        update_kernel,
        out_shape=(shape(8192, 128), shape(1024, 128), shape(8, 128), shape(2)),
        in_specs=[smem] + [vmem] * KEPT + [far] * (8 - KEPT) + [vmem] * 6,
        out_specs=(hbm, hbm, vmem, smem),
        scratch_shapes=[
            pltpu.VMEM((8192, 128), F32),
            pltpu.VMEM((1024, 128), F32),
            pltpu.VMEM((8 - KEPT, 1024, 128), F32),
            pltpu.SemaphoreType.DMA((8 - KEPT,)),
            pltpu.SemaphoreType.DMA((8,)),
            pltpu.SemaphoreType.DMA,
        ],
        compiler_params=pltpu.CompilerParams(vmem_limit_bytes=12 * MIB),
        name="update",
    )(*args)


def on_device(
    panel_index,
    coords,
    region_ids,
    nugget,
    variance,
    length,
    correction,
    bin_index,
    fraction,
    weights,
):
    coords = coords.reshape(2, 8, 128)
    args = (
        panel_index,
        nugget,
        variance,
        length,
        coords,
        region_ids.reshape(8, 128),
        bin_index.reshape(8, 8),
        fraction.reshape(8, 8),
        weights.reshape(8, 8),
        correction.reshape(8192, 128),
    )
    branches = [functools.partial(exchange, d) for d in range(N)]
    moved = lax.switch(panel_index[0] & (N - 1), branches, *args)
    trailing, panel, scores, terms = update(panel_index, *moved)
    return (
        trailing.reshape(8, 1, 128, 8, 1, 128),
        panel.reshape(8, 1, 128, 128),
        scores.reshape(8, 1, 128),
        terms,
    )


def solution(mesh):
    in_specs = (
        P(),
        P(None, None, "row", None),
        P(None, "row", None),
        P(),
        P(),
        P(),
        P(None, "row", None, None, "col", None),
        P(None, "row", "col", None),
        P(None, "row", "col", None),
        P(None, "row", "col", None),
    )
    out_specs = (
        P(None, "row", None, None, "col", None),
        P(None, "row", None, None),
        P(None, "row", None),
        P(),
    )
    return jax.shard_map(
        on_device, mesh=mesh, in_specs=in_specs, out_specs=out_specs, check_vma=False
    )
```

```python
import functools

import jax
import jax.numpy as jnp
from jax import lax
from jax.experimental import pallas as pl
from jax.experimental.pallas import tpu as pltpu
from jax.sharding import PartitionSpec as P

F32 = jnp.float32
BF16 = jnp.bfloat16
I32 = jnp.int32
MESH = pl.DeviceIdType.MESH
N = 16
NREG = 16
ROOT_THREE = 1.7320508075688772
ROOT_TWO = 1.4142135623730951
NT = (((1,), (1,)), ((), ()))
NN = (((1,), (0,)), ((), ()))
TN = (((0,), (0,)), ((), ()))
PIECE = 64
MIDDLE = 3
EARLY = 2
KEPT = 4
MIB = 2**20


def iota(shape, dim):
    return lax.broadcasted_iota(I32, shape, dim)


def split2(x):
    high = x.astype(BF16)
    return high, (x - high.astype(F32)).astype(BF16)


def split3(x):
    high = x.astype(BF16)
    rest = x - high.astype(F32)
    mid = rest.astype(BF16)
    return high, mid, (rest - mid.astype(F32)).astype(BF16)


def dot3(a, b, dims):
    (ca,), (cb,) = dims[0]
    ah, al = split2(a)
    bh, bl = split2(b)
    return lax.dot_general(
        jnp.concatenate([ah, ah, al], axis=ca),
        jnp.concatenate([bh, bl, bh], axis=cb),
        dims,
        preferred_element_type=F32,
    )


def matern(dx, dy, variance):
    scaled = jnp.sqrt(dx * dx + dy * dy)
    return (variance + variance * scaled) * jnp.exp(-scaled)


def factor_inverse(work, inv, start, stop):
    nb = 16
    groups = nb // 8
    sub = iota((8, 128), 0)
    lane = iota((nb, 128), 1)

    def block(p, carry):
        rows_k = [work[8 * g : 8 * g + 8, :] for g in range(groups)]
        rows_i = [inv[8 * g : 8 * g + 8, :] for g in range(groups)]
        col = [
            [
                jnp.broadcast_to(rows_k[g][:, q : q + 1], (8, 128)) if 8 * g + 7 >= q else None
                for g in range(groups)
            ]
            for q in range(nb)
        ]
        pivots = [jnp.ones((8, 128), F32) for _ in range(groups)]
        for j in range(nb):
            gj, sj = divmod(j, 8)
            pivot = jnp.broadcast_to(col[j][gj][sj : sj + 1, :], (8, 128))
            pivots[gj] = jnp.where(sub == sj, pivot, pivots[gj])
            if j == nb - 1:
                break
            recip = 1.0 / pivot
            mult = [None] * groups
            for g in range(gj, groups):
                m = col[j][g] * recip
                mult[g] = jnp.where(sub > sj, m, 0.0) if g == gj else m
            for q in range(j + 1, nb):
                gq, sq = divmod(q, 8)
                scale = jnp.broadcast_to(col[j][gq][sq : sq + 1, :], (8, 128))
                for g in range(gq, groups):
                    col[q][g] = col[q][g] - mult[g] * scale
            row_k = jnp.broadcast_to(rows_k[gj][sj : sj + 1, :], (8, 128))
            row_i = jnp.broadcast_to(rows_i[gj][sj : sj + 1, :], (8, 128))
            for g in range(gj, groups):
                if 8 * g + 7 > j:
                    rows_k[g] = rows_k[g] - mult[g] * row_k
                    rows_i[g] = rows_i[g] - mult[g] * row_i
        roots = [lax.rsqrt(x) for x in pivots]
        upper = jnp.concatenate([rows_k[g] * roots[g] for g in range(groups)], axis=0)
        done = jnp.concatenate([rows_i[g] * roots[g] for g in range(groups)], axis=0)
        below = jnp.where((lane >= nb) & (lane < 128 - nb * p), upper, 0.0)
        h, m, l = split3(below)
        h2, m2, l2 = split3(done)
        left = jnp.concatenate([h, h, m, m, h, l], axis=0)
        right = jnp.concatenate(
            [
                jnp.concatenate([h, m, h, m, l, h], axis=0),
                jnp.concatenate([h2, m2, h2, m2, l2, h2], axis=0),
            ],
            axis=1,
        )
        update = lax.dot_general(left, right, TN, preferred_element_type=F32)
        next_k = work[nb:, :] - update[nb:, :128]
        next_i = inv[nb:, :] - update[nb:, 128:]
        work[0 : 128 - nb, :] = pltpu.roll(next_k, 128 - nb, 1)
        inv[0 : 128 - nb, :] = next_i
        inv[128 - nb :, :] = done
        return carry

    lax.fori_loop(start, stop, block, 0)


def exchange_kernel(
    d,
    k_hbm,
    nugget_hbm,
    variance_hbm,
    length_hbm,
    coords_hbm,
    regions_hbm,
    bins_hbm,
    fraction_hbm,
    weights_hbm,
    corr_hbm,
    *refs,
):
    matrix_out = refs[:8]
    exchange_body(
        d,
        (
            k_hbm,
            nugget_hbm,
            variance_hbm,
            length_hbm,
            coords_hbm,
            regions_hbm,
            bins_hbm,
            fraction_hbm,
            weights_hbm,
        ),
        corr_hbm,
        matrix_out,
        *refs[8:],
    )


def exchange_body(
    d,
    small_hbm,
    corr_hbm,
    matrix_out,
    rows_out,
    cols_out,
    inverse_out,
    hist_out,
    sites_out,
    pivot_out,
    k_ref,
    nugget_ref,
    variance_ref,
    length_ref,
    coords_s,
    coords_ref,
    regions_ref,
    bins_ref,
    fraction_ref,
    weights_ref,
    corr,
    row_raw,
    col_raw,
    work,
    inverse,
    factor_rx,
    col_sites,
    pivot_info,
    hist,
    hist_rx,
    hist_sum,
    hist_rx2,
    hist_all,
    pivot_obs,
    in_sem,
    small_sem,
    out_sem,
    send,
    recv,
    row_recv,
):
    (
        k_hbm,
        nugget_hbm,
        variance_hbm,
        length_hbm,
        coords_hbm,
        regions_hbm,
        bins_hbm,
        fraction_hbm,
        weights_hbm,
    ) = small_hbm
    r = lax.axis_index("row")
    c = lax.axis_index("col")
    sibling = c + 1 - 2 * lax.rem(c, 2)
    (
        S_SITES, S_PIVOT, S_OBS, S_F1, S_F2, S_F3, S_H2, S_H3, S_PO, S_R1, S_R2, S_R3, S_C1, S_C2, S_H1,
    ) = range(15)

    def row_peer(i):
        return lax.rem(r + i, N)

    def col_peer(i):
        return lax.rem(c + i, N)

    def send_to(src, dst, which, to, sem=None):
        pltpu.make_async_remote_copy(
            src_ref=src,
            dst_ref=dst,
            send_sem=send.at[which],
            recv_sem=recv.at[which] if sem is None else sem,
            device_id=to,
            device_id_type=MESH,
        ).start()

    def wait(ref, sem):
        pltpu.make_async_copy(ref, ref, sem).wait()

    def each_peer(body):
        def step(i, carry):
            body(i)
            return carry

        lax.fori_loop(1, N, step, 0)

    def rows8(ref, i):
        return ref.at[pl.ds(pl.multiple_of(i * 8, 8), 8)]

    def piece(ref, i):
        return ref.at[pl.ds(pl.multiple_of(i * PIECE, PIECE), PIECE)]

    barrier = pltpu.get_barrier_semaphore()

    def greet(i):
        pl.semaphore_signal(barrier, inc=1, device_id=(row_peer(i), c), device_id_type=MESH)
        pl.semaphore_signal(barrier, inc=1, device_id=(r, col_peer(i)), device_id_type=MESH)

    each_peer(greet)
    load = pltpu.make_async_copy(corr_hbm, corr, in_sem)
    small = [
        pltpu.make_async_copy(src, dst, small_sem.at[i])
        for i, (src, dst) in enumerate(
            (
                (coords_hbm, coords_s),
                (coords_hbm, coords_ref),
                (regions_hbm, regions_ref),
                (bins_hbm, bins_ref),
                (fraction_hbm, fraction_ref),
                (weights_hbm, weights_ref),
                (k_hbm, k_ref),
                (nugget_hbm, nugget_ref),
                (variance_hbm, variance_ref),
                (length_hbm, length_ref),
            )
        )
    ]
    for copy in small:
        copy.start()
    load.start()
    for copy in small:
        copy.wait()

    tile_at = jnp.full((128, 128), k_ref[0] // N, I32)
    factor = ROOT_THREE / length_ref[0]
    variance = variance_ref[0]
    regions = regions_ref[...]
    nugget = jnp.zeros((8, 128), F32)
    for g in range(NREG):
        nugget = jnp.where(regions == g, nugget_ref[g], nugget)
    obs = jnp.concatenate(
        [bins_ref[...].astype(F32), fraction_ref[...], weights_ref[...], jnp.zeros((8, 104), F32)],
        axis=1,
    )
    lane = iota((8, 128), 1)
    level = iota((128, 128), 0)

    def one_row(x):
        spread = pltpu.roll(x, 0, 1, stride=8, stride_axis=0)
        return jnp.sum(jnp.where(lane // 8 == iota((8, 128), 0), spread, 0.0), axis=0, keepdims=True)

    own_bins_f = one_row(obs)
    own_fraction = one_row(pltpu.roll(obs, 128 - 8, 1))
    own_weights = one_row(pltpu.roll(obs, 128 - 16, 1))
    own_bins = own_bins_f.astype(I32)
    weighted = jnp.where(level == (own_bins // 256) * 8 + (own_bins // 128) % 2, own_weights, 0.0)
    wh, wl = split2(weighted)
    low = (level == own_bins % 128).astype(F32).astype(BF16)
    counts = lax.dot_general(
        jnp.concatenate([wh, wl], axis=1),
        jnp.concatenate([low, low], axis=1),
        NT,
        preferred_element_type=F32,
    )
    own_row = jnp.where(lane[0:1] < 64, own_bins_f, pltpu.roll(jnp.broadcast_to(own_fraction, (8, 128)), 64, 1)[0:1])
    hist[...] = jnp.where(level % 8 == 2, own_row, counts)

    pad = jnp.zeros((120, 128), F32)
    x_rows = jnp.transpose(jnp.concatenate([coords_ref[0], pad], axis=0)) * factor
    y_rows = jnp.transpose(jnp.concatenate([coords_ref[1], pad], axis=0)) * factor
    diagonal = iota((128, 128), 0) == iota((128, 128), 1)

    def pick_row(x):
        return jnp.sum(jnp.where(iota((8, 128), 0) == tile_at[0:8], x, 0.0), axis=0, keepdims=True)

    def pick(tiles, rows):
        found = tiles(0)
        for b in range(1, 8):
            found = jnp.where(tile_at[0:rows] == b, tiles(b), found)
        return found

    @pl.when(r == d)
    def _():
        pivot_info[...] = jnp.concatenate(
            [
                pick_row(coords_ref[0]),
                pick_row(coords_ref[1]),
                pick_row(nugget),
                jnp.zeros((5, 128), F32),
            ],
            axis=0,
        )

    load.wait()

    @pl.when(c == d)
    def _():
        def rows_of(i, carry):
            row_raw[pl.ds(pl.multiple_of(i * 32, 32), 32), :] = pick(
                lambda b: corr[pl.ds(i * 256 + b, 32, stride=8), :], 32
            )
            return carry

        lax.fori_loop(0, 32, rows_of, 0)

    @pl.when(r == d)
    def _():
        def cols_of(i, carry):
            at = pl.multiple_of(i * 32, 32)
            col_raw[pl.ds(at, 32), :] = pick(lambda b: corr[pl.ds(b * 1024 + at, 32), :], 32)
            return carry

        lax.fori_loop(0, 32, cols_of, 0)

    @pl.when((r == d) & (c == d))
    def _():
        info = pivot_info[...]
        across = jnp.transpose(info)
        px = info[0:1, :] * factor
        py = info[1:2, :] * factor
        tile = matern(across[:, 0:1] * factor - px, across[:, 1:2] * factor - py, variance)
        work[...] = tile + jnp.where(diagonal, info[2:3, :], 0.0)

        def own_tile(i, carry):
            at = pl.ds(pl.multiple_of(i * 32, 32), 32)
            work[at, :] = work[at, :] - pick(lambda b: row_raw[pl.ds(b * 128 + i * 32, 32), :], 32)
            return carry

        lax.fori_loop(0, 4, own_tile, 0)
        inverse[...] = jnp.where(diagonal, 1.0, 0.0)

    def half(stage, carry):
        @pl.when((r == d) & (c == d))
        def _():
            factor_inverse(work, inverse, 4 * stage, 4 * stage + 4)

        @pl.when(stage == 0)
        def _():
            first_sends()

        return carry

    def first_sends():
        pl.semaphore_wait(barrier, 2 * (N - 1))

        @pl.when(r == d)
        def _():
            each_peer(
                lambda i: send_to(
                    piece(col_raw, row_peer(i)), piece(col_raw, row_peer(i)), S_C1, (row_peer(i), c)
                )
            )

        each_peer(lambda i: send_to(rows8(hist, col_peer(i)), hist_rx.at[i], S_H1, (r, col_peer(i))))

        @pl.when(c == d)
        def _():
            each_peer(
                lambda i: send_to(
                    piece(row_raw, col_peer(i)), piece(row_raw, col_peer(i)), S_R1, (r, col_peer(i))
                )
            )

        @pl.when(r == c)
        def _():
            each_peer(lambda i: send_to(coords_ref, col_sites, S_SITES, (row_peer(i), c)))
            col_sites[...] = coords_ref[...]

        @pl.when(r == d)
        def _():
            each_peer(lambda i: send_to(pivot_info, pivot_info, S_PIVOT, (row_peer(i), c)))

    lax.fori_loop(0, 2, half, 0)

    @pl.when((r == d) & (c == d))
    def _():
        factor_rx[8 * d : 8 * d + 8, :] = inverse[8 * d : 8 * d + 8, :]
        each_peer(
            lambda i: send_to(
                rows8(inverse, col_peer(i)), rows8(factor_rx, col_peer(i)), S_F1, (r, col_peer(i))
            )
        )

    @pl.when((r == d) & (c != d))
    def _():
        wait(rows8(factor_rx, c), recv.at[S_F1])

    @pl.when(r == d)
    def _():
        each_peer(
            lambda i: send_to(rows8(factor_rx, c), rows8(factor_rx, c), S_F2, (row_peer(i), c))
        )

    def share_row(i, carry):
        to = col_peer(2 * i)

        @pl.when(to != d)
        def _():
            send_to(piece(row_raw, c), piece(row_raw, c), S_R2, (r, to), row_recv.at[c // 2])

        return carry

    @pl.when(c != d)
    def _():
        wait(piece(row_raw, c), recv.at[S_R1])

    lax.fori_loop(1, 8, share_row, 0)

    @pl.when(sibling != d)
    def _():
        send_to(piece(row_raw, c), piece(row_raw, c), S_R3, (r, sibling))

    wait(hist_rx.at[pl.ds(1, 15)], recv.at[S_H1])
    own = pl.ds(pl.multiple_of(c * 8, 8), 8)
    summed = lax.fori_loop(1, N, lambda i, total: total + hist_rx[i], hist[own, :])
    hist_sum[...] = jnp.where(iota((8, 128), 0) < 2, summed, 0.0)
    each_peer(lambda i: send_to(hist_sum, hist_rx2.at[i], S_H2, (row_peer(i), c)))

    @pl.when(r != c)
    def _():
        wait(col_sites, recv.at[S_SITES])

    col_x = col_sites[0] * factor
    col_y = col_sites[1] * factor
    place = iota((8, 128), 0) * 128 + lane
    own_nugget = jnp.where(r == c, nugget, 0.0)

    def form(a):
        def eight(q, carry):
            for u in range(8):
                t = q * 8 + u
                at = pl.ds(pl.multiple_of(a * 1024 + t * 8, 8), 8)
                value = matern(
                    coords_s[0, a, t] * factor - col_x, coords_s[1, a, t] * factor - col_y, variance
                )
                value = value + jnp.where(place == a * 128 + t, own_nugget, 0.0)
                corr[at, :] = value - corr[at, :]
            return carry

        lax.fori_loop(0, 16, eight, 0)
        for b in range(8):

            @pl.when(a == b)
            def _():
                at = pl.ds(b * 1024, 1024)
                pltpu.make_async_copy(corr.at[at], matrix_out[b], out_sem).start()

    lax.fori_loop(0, EARLY, lambda a, carry: (form(a), carry)[1], 0)

    @pl.when(r != d)
    def _():
        wait(piece(col_raw, r), recv.at[S_C1])

    def share_col(i):
        @pl.when(row_peer(i) != d)
        def _():
            send_to(piece(col_raw, r), piece(col_raw, r), S_C2, (row_peer(i), c))

    each_peer(share_col)

    hist_rx[0] = hist[own, :]

    def unpack(i, found):
        source = lax.rem(c - i + N, N)
        packed = jnp.broadcast_to(hist_rx[i][2:3, :], (8, 128))
        spread = pltpu.roll(packed, 0, 1, stride=8, stride_axis=0)
        here = (lane // 8) == source
        return tuple(
            jnp.where(
                here,
                pltpu.roll(spread, lax.rem(8 * source + 64 * j + 72, 128), 1),
                found[j],
            )
            for j in range(2)
        )

    found = lax.fori_loop(0, N, unpack, (jnp.zeros((8, 128), F32), jnp.zeros((8, 128), F32)))
    found = [jnp.concatenate([x[7 - a : 8 - a] for a in range(8)], axis=0) for x in found]
    for j in range(2):
        sites_out[j] = found[j]

    @pl.when(r == d)
    def _():
        pivot_obs[...] = jnp.concatenate(
            [pick_row(found[0]), pick_row(found[1]), jnp.zeros((6, 128), F32)], axis=0
        )
        each_peer(lambda i: send_to(pivot_obs, pivot_obs, S_PO, (row_peer(i), c)))

    def pass_on(i):
        source = lax.rem(c + 16 - 2 * i, N)
        wait(piece(row_raw, source), row_recv.at[source // 2])

        @pl.when(sibling != d)
        def _():
            send_to(piece(row_raw, source), piece(row_raw, source), S_R3, (r, sibling))

    def pass_own(i):
        source = lax.rem(c + 16 - 2 * i, N)
        send_to(piece(row_raw, source), piece(row_raw, source), S_R3, (r, sibling))

    def pass_piece(i):
        @pl.when(c != d)
        def _():
            pass_on(i)

        @pl.when(c == d)
        def _():
            pass_own(i)

    def form_and_pass(a, carry):
        form(a)
        pass_piece(a - 1)
        return carry

    def later(a, carry):
        @pl.when(a == MIDDLE)
        def _():
            last_hops()

        form_and_pass(a, carry)
        return carry

    def last_hops():
        @pl.when(r != d)
        def _():
            wait(rows8(factor_rx, c), recv.at[S_F2])

        each_peer(lambda i: send_to(rows8(factor_rx, c), rows8(factor_rx, c), S_F3, (r, col_peer(i))))

        wait(hist_rx2.at[pl.ds(1, 15)], recv.at[S_H2])
        hist_all[own, :] = lax.fori_loop(
            1, N, lambda i, total: total + hist_rx2[i], hist_sum[...]
        )
        each_peer(
            lambda i: send_to(rows8(hist_all, c), rows8(hist_all, c), S_H3, (r, col_peer(i)))
        )

    lax.fori_loop(EARLY, 8, later, 0)
    pass_piece(7)

    @pl.when(r != d)
    def _():
        wait(pivot_info, recv.at[S_PIVOT])

    info = pivot_info[...]
    across = jnp.transpose(info)
    px = info[0:1, :] * factor
    py = info[1:2, :] * factor
    pnug = jnp.where(diagonal, info[2:3, :], 0.0)
    tx = across[:, 0:1] * factor
    ty = across[:, 1:2] * factor

    def panels(a, carry):
        at = pl.ds(pl.multiple_of(a * 128, 128), 128)
        turn = lax.rem(128 - a, 128)
        x = pltpu.roll(x_rows, turn, 1)[:, 0:1]
        y = pltpu.roll(y_rows, turn, 1)[:, 0:1]
        extra = jnp.where(tile_at == a, pnug, 0.0)
        rows_out[at, :] = matern(x - px, y - py, variance) + jnp.where(r == d, extra, 0.0)
        x = col_sites[0, pl.ds(a, 1), :] * factor
        y = col_sites[1, pl.ds(a, 1), :] * factor
        cols_out[a] = matern(tx - x, ty - y, variance) + jnp.where(c == d, extra, 0.0)
        return carry

    lax.fori_loop(0, 8, panels, 0)

    @pl.when(r != d)
    def _():
        wait(col_raw.at[pl.ds(0, 15 * PIECE)], recv.at[S_C2])
        wait(pivot_obs, recv.at[S_PO])


    def less_cols(b, carry):
        cols_out[b] = cols_out[b] - col_raw[pl.ds(b, 128, stride=8), :]
        return carry

    lax.fori_loop(0, 8, less_cols, 0)
    pivot_out[...] = pivot_obs[...]
    wait(factor_rx.at[pl.ds(0, 120)], recv.at[S_F3])
    inverse_out[...] = factor_rx[...]
    wait(hist_all.at[pl.ds(0, 120)], recv.at[S_H3])
    hist_out[...] = hist_all[...]

    @pl.when(c != d)
    def _():
        wait(row_raw.at[pl.ds(0, 8 * PIECE)], recv.at[S_R3])

    def less_rows(a, carry):
        at = pl.ds(pl.multiple_of(a * 128, 128), 128)
        rows_out[at, :] = rows_out[at, :] - row_raw[at, :]
        return carry

    lax.fori_loop(0, 8, less_rows, 0)

    def sent(ref, which):
        wait(ref, send.at[which])

    @pl.when(r == d)
    def _():
        sent(hist.at[pl.ds(0, 120)], S_PIVOT)
        sent(hist.at[pl.ds(0, 120)], S_F2)
        sent(hist.at[pl.ds(0, 120)], S_PO)
        sent(col_raw.at[pl.ds(0, 15 * PIECE)], S_C1)
        sent(col_raw.at[pl.ds(0, 15 * PIECE)], S_C2)

    @pl.when(r != d)
    def _():
        sent(col_raw.at[pl.ds(0, 14 * PIECE)], S_C2)

    @pl.when(r == c)
    def _():
        sent(row_raw.at[pl.ds(0, 240)], S_SITES)

    @pl.when((r == d) & (c == d))
    def _():
        sent(hist.at[pl.ds(0, 120)], S_F1)

    @pl.when(c == d)
    def _():
        sent(row_raw.at[pl.ds(0, 15 * PIECE)], S_R1)

    for which in (S_F3, S_H1, S_H2, S_H3):
        sent(hist.at[pl.ds(0, 120)], which)

    same_place = lax.rem(c, 2) == d % 2

    @pl.when(same_place & (c != d))
    def _():
        sent(row_raw.at[pl.ds(0, 6 * PIECE)], S_R2)

    @pl.when(jnp.logical_not(same_place) | (c == d))
    def _():
        sent(row_raw.at[pl.ds(0, 7 * PIECE)], S_R2)

    @pl.when(sibling != d)
    def _():
        sent(row_raw.at[pl.ds(0, 8 * PIECE)], S_R3)

    wait(corr, out_sem)


def exchange(d, *args):
    vmem = pl.BlockSpec(memory_space=pltpu.VMEM)
    hbm = pl.BlockSpec(memory_space=pl.ANY)
    far = pl.BlockSpec(memory_space=pltpu.HBM)
    shape = lambda *s: jax.ShapeDtypeStruct(s, F32)
    return pl.pallas_call(
        functools.partial(exchange_kernel, d),
        out_shape=(
            *[shape(1024, 128) for _ in range(KEPT)],
            *[pltpu.HBM((1024, 128), F32) for _ in range(8 - KEPT)],
            shape(1024, 128),
            shape(8, 128, 128),
            shape(128, 128),
            shape(128, 128),
            shape(2, 8, 128),
            shape(8, 128),
        ),
        in_specs=[hbm] * 10,
        out_specs=(vmem,) * KEPT + (far,) * (8 - KEPT) + (vmem,) * 6,
        scratch_shapes=[
            pltpu.SMEM((1,), I32),
            pltpu.SMEM((NREG,), F32),
            pltpu.SMEM((1,), F32),
            pltpu.SMEM((1,), F32),
            pltpu.SMEM((2, 8, 128), F32),
            pltpu.VMEM((2, 8, 128), F32),
            pltpu.VMEM((8, 128), I32),
            pltpu.VMEM((8, 8), I32),
            pltpu.VMEM((8, 8), F32),
            pltpu.VMEM((8, 8), F32),
            pltpu.VMEM((8192, 128), F32),
            pltpu.VMEM((1024, 128), F32),
            pltpu.VMEM((1024, 128), F32),
            pltpu.VMEM((128, 128), F32),
            pltpu.VMEM((128, 128), F32),
            pltpu.VMEM((128, 128), F32),
            pltpu.VMEM((2, 8, 128), F32),
            pltpu.VMEM((8, 128), F32),
            pltpu.VMEM((128, 128), F32),
            pltpu.VMEM((N, 8, 128), F32),
            pltpu.VMEM((8, 128), F32),
            pltpu.VMEM((N, 8, 128), F32),
            pltpu.VMEM((128, 128), F32),
            pltpu.VMEM((8, 128), F32),
            pltpu.SemaphoreType.DMA,
            pltpu.SemaphoreType.DMA((10,)),
            pltpu.SemaphoreType.DMA,
            pltpu.SemaphoreType.DMA((15,)),
            pltpu.SemaphoreType.DMA((15,)),
            pltpu.SemaphoreType.DMA((8,)),
        ],
        compiler_params=pltpu.CompilerParams(
            collective_id=d, has_side_effects=True, vmem_limit_bytes=12 * MIB
        ),
        name="exchange",
    )(*args)


def quantile(x):
    w = -jnp.log((1.0 - x) * (1.0 + x)) - 2.5
    p = jnp.full_like(w, 2.81022636e-08)
    for coefficient in (
        3.43273939e-07,
        -3.5233877e-06,
        -4.39150654e-06,
        0.00021858087,
        -0.00125372503,
        -0.00417768164,
        0.246640727,
        1.50140941,
    ):
        p = coefficient + p * w
    return p * x


def update_kernel(k_ref, *refs):
    matrix_ref = refs[:8]
    rows_ref, cols_ref, inverse_ref, hist_ref, sites_ref, pivot_ref = refs[8:14]
    trailing_hbm, panel_hbm, scores_ref, terms_ref = refs[14:18]
    trailing, panel, late, in_sem, out_sem, panel_sem = refs[18:]
    loads = [
        pltpu.make_async_copy(matrix_ref[a], late.at[a - KEPT], in_sem.at[a - KEPT])
        for a in range(KEPT, 8)
    ]
    for load in loads:
        load.start()
    inverse = inverse_ref[...]
    cols = dot3(inverse, jnp.concatenate([cols_ref[b] for b in range(8)], axis=1), NN)
    high, low = split2(cols)
    right = jnp.concatenate([high, low, high], axis=0)
    whole = dot3(rows_ref[...], inverse, NT)
    panel[...] = whole
    whole_high, whole_low = split2(whole)
    left = jnp.concatenate([whole_high, whole_high, whole_low], axis=1)

    counts = hist_ref[...]
    level = iota((128, 128), 0)
    across = iota((128, 128), 1)
    parts = split3(counts)
    ahead = (across < level).astype(F32).astype(BF16)
    earlier = (level < across).astype(F32).astype(BF16)
    above = jnp.zeros((128, 128), F32)
    along = jnp.zeros((128, 128), F32)
    for part in parts:
        above = above + lax.dot_general(ahead, part, NN, preferred_element_type=F32)
        along = along + lax.dot_general(part, earlier, NN, preferred_element_type=F32)
    before = jnp.sum(above, axis=1, keepdims=True) + along
    total = jnp.sum(jnp.sum(counts, axis=1, keepdims=True), axis=0, keepdims=True)

    bins_f = jnp.concatenate([sites_ref[0], pivot_ref[...]], axis=0)
    fraction = jnp.concatenate([sites_ref[1], pivot_ref[...]], axis=0)
    bins_i = bins_f.astype(I32)
    high_i = (bins_i // 256) * 8 + (bins_i // 128) % 2
    low_i = bins_i % 128
    high_hot = jnp.concatenate(
        [(level == high_i[i : i + 1, :]).astype(F32).astype(BF16) for i in range(9)], axis=1
    )
    tripled = jnp.concatenate([high_hot] * 3, axis=0)
    look = [
        lax.dot_general(
            jnp.concatenate(split3(table), axis=0), tripled, TN, preferred_element_type=F32
        )
        for table in (before, counts)
    ]
    probs = []
    for i in range(9):
        hot = level == low_i[i : i + 1, :]
        at = slice(i * 128, (i + 1) * 128)
        start = jnp.sum(jnp.where(hot, look[0][:, at], 0.0), axis=0, keepdims=True)
        count = jnp.sum(jnp.where(hot, look[1][:, at], 0.0), axis=0, keepdims=True)
        part = fraction[i : i + 1, :] if i < 8 else fraction[9:10, :]
        probs.append((start + part * count) / total)
    probs = jnp.concatenate(probs + [jnp.full((7, 128), 0.5, F32)], axis=0)
    found = ROOT_TWO * quantile(2.0 * jnp.clip(probs, 0.01, 0.99) - 1.0)
    z = dot3(jnp.broadcast_to(found[8:9, :], (8, 128)), inverse, NT)
    diagonal = jnp.sum(jnp.where(level == across, inverse, 0.0), axis=0, keepdims=True)
    terms_ref[0] = -2.0 * jnp.sum(jnp.log(diagonal))
    terms_ref[1] = jnp.sum(z[0:1, :] * z[0:1, :])
    moved = dot3(z, whole, NT)
    k = k_ref[0]
    here = lax.axis_index("row") == k % N
    for a in range(8):
        score = found[a : a + 1, :] - moved[0:1, a * 128 : (a + 1) * 128]
        scores_ref[a : a + 1, :] = jnp.where(here & (k // N == a), z[0:1, :], score)

    panel_copy = pltpu.make_async_copy(panel, panel_hbm, panel_sem)
    panel_copy.start()
    for a in range(8):
        change = lax.dot_general(
            left[a * 128 : (a + 1) * 128], right, NN, preferred_element_type=F32
        )
        block = matrix_ref[a] if a < KEPT else late.at[a - KEPT]
        if a >= KEPT:
            loads[a - KEPT].wait()
        for b in range(8):
            at = pl.ds(a * 1024 + b, 128, stride=8)
            before = block[pl.ds(b, 128, stride=8), :]
            trailing[at, :] = before - change[:, b * 128 : (b + 1) * 128]
        at = pl.ds(a * 1024, 1024)
        pltpu.make_async_copy(trailing.at[at], trailing_hbm.at[at], out_sem.at[a]).start()

    panel_copy.wait()
    for a in range(8):
        at = pl.ds(a * 1024, 1024)
        pltpu.make_async_copy(trailing.at[at], trailing_hbm.at[at], out_sem.at[a]).wait()


def update(*args):
    shape = lambda *s: jax.ShapeDtypeStruct(s, F32)
    vmem = pl.BlockSpec(memory_space=pltpu.VMEM)
    smem = pl.BlockSpec(memory_space=pltpu.SMEM)
    hbm = pl.BlockSpec(memory_space=pl.ANY)
    far = pl.BlockSpec(memory_space=pltpu.HBM)
    return pl.pallas_call(
        update_kernel,
        out_shape=(shape(8192, 128), shape(1024, 128), shape(8, 128), shape(2)),
        in_specs=[smem] + [vmem] * KEPT + [far] * (8 - KEPT) + [vmem] * 6,
        out_specs=(hbm, hbm, vmem, smem),
        scratch_shapes=[
            pltpu.VMEM((8192, 128), F32),
            pltpu.VMEM((1024, 128), F32),
            pltpu.VMEM((8 - KEPT, 1024, 128), F32),
            pltpu.SemaphoreType.DMA((8 - KEPT,)),
            pltpu.SemaphoreType.DMA((8,)),
            pltpu.SemaphoreType.DMA,
        ],
        compiler_params=pltpu.CompilerParams(vmem_limit_bytes=12 * MIB),
        name="update",
    )(*args)


def on_device(
    panel_index,
    coords,
    region_ids,
    nugget,
    variance,
    length,
    correction,
    bin_index,
    fraction,
    weights,
):
    coords = coords.reshape(2, 8, 128)
    args = (
        panel_index,
        nugget,
        variance,
        length,
        coords,
        region_ids.reshape(8, 128),
        bin_index.reshape(8, 8),
        fraction.reshape(8, 8),
        weights.reshape(8, 8),
        correction.reshape(8192, 128),
    )
    branches = [functools.partial(exchange, d) for d in range(N)]
    moved = lax.switch(panel_index[0] & (N - 1), branches, *args)
    trailing, panel, scores, terms = update(panel_index, *moved)
    return (
        trailing.reshape(8, 1, 128, 8, 1, 128),
        panel.reshape(8, 1, 128, 128),
        scores.reshape(8, 1, 128),
        terms,
    )


def solution(mesh):
    in_specs = (
        P(),
        P(None, None, "row", None),
        P(None, "row", None),
        P(),
        P(),
        P(),
        P(None, "row", None, None, "col", None),
        P(None, "row", "col", None),
        P(None, "row", "col", None),
        P(None, "row", "col", None),
    )
    out_specs = (
        P(None, "row", None, None, "col", None),
        P(None, "row", None, None),
        P(None, "row", None),
        P(),
    )
    return jax.shard_map(
        on_device, mesh=mesh, in_specs=in_specs, out_specs=out_specs, check_vma=False
    )
```

```python
import functools

import jax
import jax.numpy as jnp
from jax import lax
from jax.experimental import pallas as pl
from jax.experimental.pallas import tpu as pltpu
from jax.sharding import PartitionSpec as P

F32 = jnp.float32
BF16 = jnp.bfloat16
I32 = jnp.int32
MESH = pl.DeviceIdType.MESH
N = 16
NREG = 16
ROOT_THREE = 1.7320508075688772
ROOT_TWO = 1.4142135623730951
NT = (((1,), (1,)), ((), ()))
NN = (((1,), (0,)), ((), ()))
TN = (((0,), (0,)), ((), ()))
PIECE = 64
MIDDLE = 3
EARLY = 2
KEPT = 4
MIB = 2**20


def iota(shape, dim):
    return lax.broadcasted_iota(I32, shape, dim)


def split2(x):
    high = x.astype(BF16)
    return high, (x - high.astype(F32)).astype(BF16)


def split3(x):
    high = x.astype(BF16)
    rest = x - high.astype(F32)
    mid = rest.astype(BF16)
    return high, mid, (rest - mid.astype(F32)).astype(BF16)


def dot3(a, b, dims):
    (ca,), (cb,) = dims[0]
    ah, al = split2(a)
    bh, bl = split2(b)
    return lax.dot_general(
        jnp.concatenate([ah, ah, al], axis=ca),
        jnp.concatenate([bh, bl, bh], axis=cb),
        dims,
        preferred_element_type=F32,
    )


def matern(dx, dy, variance):
    scaled = jnp.sqrt(dx * dx + dy * dy)
    return (variance + variance * scaled) * jnp.exp(-scaled)


def factor_inverse(work, inv, start, stop):
    nb = 16
    groups = nb // 8
    sub = iota((8, 128), 0)
    lane = iota((nb, 128), 1)

    def block(p, carry):
        rows_k = [work[8 * g : 8 * g + 8, :] for g in range(groups)]
        rows_i = [inv[8 * g : 8 * g + 8, :] for g in range(groups)]
        col = [
            [
                jnp.broadcast_to(rows_k[g][:, q : q + 1], (8, 128)) if 8 * g + 7 >= q else None
                for g in range(groups)
            ]
            for q in range(nb)
        ]
        pivots = [jnp.ones((8, 128), F32) for _ in range(groups)]
        for j in range(nb):
            gj, sj = divmod(j, 8)
            pivot = jnp.broadcast_to(col[j][gj][sj : sj + 1, :], (8, 128))
            pivots[gj] = jnp.where(sub == sj, pivot, pivots[gj])
            if j == nb - 1:
                break
            recip = 1.0 / pivot
            mult = [None] * groups
            for g in range(gj, groups):
                m = col[j][g] * recip
                mult[g] = jnp.where(sub > sj, m, 0.0) if g == gj else m
            for q in range(j + 1, nb):
                gq, sq = divmod(q, 8)
                scale = jnp.broadcast_to(col[j][gq][sq : sq + 1, :], (8, 128))
                for g in range(gq, groups):
                    col[q][g] = col[q][g] - mult[g] * scale
            row_k = jnp.broadcast_to(rows_k[gj][sj : sj + 1, :], (8, 128))
            row_i = jnp.broadcast_to(rows_i[gj][sj : sj + 1, :], (8, 128))
            for g in range(gj, groups):
                if 8 * g + 7 > j:
                    rows_k[g] = rows_k[g] - mult[g] * row_k
                    rows_i[g] = rows_i[g] - mult[g] * row_i
        roots = [lax.rsqrt(x) for x in pivots]
        upper = jnp.concatenate([rows_k[g] * roots[g] for g in range(groups)], axis=0)
        done = jnp.concatenate([rows_i[g] * roots[g] for g in range(groups)], axis=0)
        below = jnp.where((lane >= nb) & (lane < 128 - nb * p), upper, 0.0)
        h, m, l = split3(below)
        h2, m2, l2 = split3(done)
        left = jnp.concatenate([h, h, m, m, h, l], axis=0)
        right = jnp.concatenate(
            [
                jnp.concatenate([h, m, h, m, l, h], axis=0),
                jnp.concatenate([h2, m2, h2, m2, l2, h2], axis=0),
            ],
            axis=1,
        )
        update = lax.dot_general(left, right, TN, preferred_element_type=F32)
        next_k = work[nb:, :] - update[nb:, :128]
        next_i = inv[nb:, :] - update[nb:, 128:]
        work[0 : 128 - nb, :] = pltpu.roll(next_k, 128 - nb, 1)
        inv[0 : 128 - nb, :] = next_i
        inv[128 - nb :, :] = done
        return carry

    lax.fori_loop(start, stop, block, 0)


def exchange_kernel(
    d,
    k_hbm,
    nugget_hbm,
    variance_hbm,
    length_hbm,
    coords_hbm,
    regions_hbm,
    bins_hbm,
    fraction_hbm,
    weights_hbm,
    corr_hbm,
    *refs,
):
    matrix_out = refs[:8]
    exchange_body(
        d,
        (
            k_hbm,
            nugget_hbm,
            variance_hbm,
            length_hbm,
            coords_hbm,
            regions_hbm,
            bins_hbm,
            fraction_hbm,
            weights_hbm,
        ),
        corr_hbm,
        matrix_out,
        *refs[8:],
    )


def exchange_body(
    d,
    small_hbm,
    corr_hbm,
    matrix_out,
    rows_out,
    cols_out,
    inverse_out,
    hist_out,
    sites_out,
    pivot_out,
    k_ref,
    nugget_ref,
    variance_ref,
    length_ref,
    coords_s,
    coords_ref,
    regions_ref,
    bins_ref,
    fraction_ref,
    weights_ref,
    corr,
    row_raw,
    col_raw,
    work,
    inverse,
    factor_rx,
    col_sites,
    pivot_info,
    hist,
    hist_rx,
    hist_sum,
    hist_rx2,
    hist_all,
    pivot_obs,
    in_sem,
    small_sem,
    out_sem,
    send,
    recv,
    row_recv,
):
    (
        k_hbm,
        nugget_hbm,
        variance_hbm,
        length_hbm,
        coords_hbm,
        regions_hbm,
        bins_hbm,
        fraction_hbm,
        weights_hbm,
    ) = small_hbm
    r = lax.axis_index("row")
    c = lax.axis_index("col")
    sibling = c + 1 - 2 * lax.rem(c, 2)
    (
        S_SITES, S_PIVOT, S_OBS, S_F1, S_F2, S_F3, S_H2, S_H3, S_PO, S_R1, S_R2, S_R3, S_C1, S_C2, S_H1,
    ) = range(15)

    def row_peer(i):
        return lax.rem(r + i, N)

    def col_peer(i):
        return lax.rem(c + i, N)

    def send_to(src, dst, which, to, sem=None):
        pltpu.make_async_remote_copy(
            src_ref=src,
            dst_ref=dst,
            send_sem=send.at[which],
            recv_sem=recv.at[which] if sem is None else sem,
            device_id=to,
            device_id_type=MESH,
        ).start()

    def wait(ref, sem):
        pltpu.make_async_copy(ref, ref, sem).wait()

    def each_peer(body):
        def step(i, carry):
            body(i)
            return carry

        lax.fori_loop(1, N, step, 0)

    def rows8(ref, i):
        return ref.at[pl.ds(pl.multiple_of(i * 8, 8), 8)]

    def piece(ref, i):
        return ref.at[pl.ds(pl.multiple_of(i * PIECE, PIECE), PIECE)]

    barrier = pltpu.get_barrier_semaphore()

    def greet(i):
        pl.semaphore_signal(barrier, inc=1, device_id=(row_peer(i), c), device_id_type=MESH)
        pl.semaphore_signal(barrier, inc=1, device_id=(r, col_peer(i)), device_id_type=MESH)

    each_peer(greet)
    load = pltpu.make_async_copy(corr_hbm, corr, in_sem)
    small = [
        pltpu.make_async_copy(src, dst, small_sem.at[i])
        for i, (src, dst) in enumerate(
            (
                (coords_hbm, coords_s),
                (coords_hbm, coords_ref),
                (regions_hbm, regions_ref),
                (bins_hbm, bins_ref),
                (fraction_hbm, fraction_ref),
                (weights_hbm, weights_ref),
                (k_hbm, k_ref),
                (nugget_hbm, nugget_ref),
                (variance_hbm, variance_ref),
                (length_hbm, length_ref),
            )
        )
    ]
    for copy in small:
        copy.start()
    load.start()
    for copy in small:
        copy.wait()

    tile_at = jnp.full((128, 128), k_ref[0] // N, I32)
    factor = ROOT_THREE / length_ref[0]
    variance = variance_ref[0]
    regions = regions_ref[...]
    nugget = jnp.zeros((8, 128), F32)
    for g in range(NREG):
        nugget = jnp.where(regions == g, nugget_ref[g], nugget)
    obs = jnp.concatenate(
        [bins_ref[...].astype(F32), fraction_ref[...], weights_ref[...], jnp.zeros((8, 104), F32)],
        axis=1,
    )
    lane = iota((8, 128), 1)
    level = iota((128, 128), 0)

    def one_row(x):
        spread = pltpu.roll(x, 0, 1, stride=8, stride_axis=0)
        return jnp.sum(jnp.where(lane // 8 == iota((8, 128), 0), spread, 0.0), axis=0, keepdims=True)

    own_bins_f = one_row(obs)
    own_fraction = one_row(pltpu.roll(obs, 128 - 8, 1))
    own_weights = one_row(pltpu.roll(obs, 128 - 16, 1))
    own_bins = own_bins_f.astype(I32)
    weighted = jnp.where(level == (own_bins // 256) * 8 + (own_bins // 128) % 2, own_weights, 0.0)
    wh, wl = split2(weighted)
    low = (level == own_bins % 128).astype(F32).astype(BF16)
    counts = lax.dot_general(
        jnp.concatenate([wh, wl], axis=1),
        jnp.concatenate([low, low], axis=1),
        NT,
        preferred_element_type=F32,
    )
    own_row = jnp.where(lane[0:1] < 64, own_bins_f, pltpu.roll(jnp.broadcast_to(own_fraction, (8, 128)), 64, 1)[0:1])
    hist[...] = jnp.where(level % 8 == 2, own_row, counts)

    pad = jnp.zeros((120, 128), F32)
    x_rows = jnp.transpose(jnp.concatenate([coords_ref[0], pad], axis=0)) * factor
    y_rows = jnp.transpose(jnp.concatenate([coords_ref[1], pad], axis=0)) * factor
    diagonal = iota((128, 128), 0) == iota((128, 128), 1)

    def pick_row(x):
        return jnp.sum(jnp.where(iota((8, 128), 0) == tile_at[0:8], x, 0.0), axis=0, keepdims=True)

    def pick(tiles, rows):
        found = tiles(0)
        for b in range(1, 8):
            found = jnp.where(tile_at[0:rows] == b, tiles(b), found)
        return found

    @pl.when(r == d)
    def _():
        pivot_info[...] = jnp.concatenate(
            [
                pick_row(coords_ref[0]),
                pick_row(coords_ref[1]),
                pick_row(nugget),
                jnp.zeros((5, 128), F32),
            ],
            axis=0,
        )

    load.wait()

    @pl.when(c == d)
    def _():
        def rows_of(i, carry):
            row_raw[pl.ds(pl.multiple_of(i * 32, 32), 32), :] = pick(
                lambda b: corr[pl.ds(i * 256 + b, 32, stride=8), :], 32
            )
            return carry

        lax.fori_loop(0, 32, rows_of, 0)

    @pl.when(r == d)
    def _():
        def cols_of(i, carry):
            at = pl.multiple_of(i * 32, 32)
            col_raw[pl.ds(at, 32), :] = pick(lambda b: corr[pl.ds(b * 1024 + at, 32), :], 32)
            return carry

        lax.fori_loop(0, 32, cols_of, 0)

    @pl.when((r == d) & (c == d))
    def _():
        info = pivot_info[...]
        across = jnp.transpose(info)
        px = info[0:1, :] * factor
        py = info[1:2, :] * factor
        tile = matern(across[:, 0:1] * factor - px, across[:, 1:2] * factor - py, variance)
        work[...] = tile + jnp.where(diagonal, info[2:3, :], 0.0)

        def own_tile(i, carry):
            at = pl.ds(pl.multiple_of(i * 32, 32), 32)
            work[at, :] = work[at, :] - pick(lambda b: row_raw[pl.ds(b * 128 + i * 32, 32), :], 32)
            return carry

        lax.fori_loop(0, 4, own_tile, 0)
        inverse[...] = jnp.where(diagonal, 1.0, 0.0)

    def half(stage, carry):
        @pl.when((r == d) & (c == d))
        def _():
            factor_inverse(work, inverse, 4 * stage, 4 * stage + 4)

        @pl.when(stage == 0)
        def _():
            first_sends()

        return carry

    def first_sends():
        pl.semaphore_wait(barrier, 2 * (N - 1))

        @pl.when(r == d)
        def _():
            each_peer(
                lambda i: send_to(
                    piece(col_raw, row_peer(i)), piece(col_raw, row_peer(i)), S_C1, (row_peer(i), c)
                )
            )

        each_peer(lambda i: send_to(rows8(hist, col_peer(i)), hist_rx.at[i], S_H1, (r, col_peer(i))))

        @pl.when(c == d)
        def _():
            each_peer(
                lambda i: send_to(
                    piece(row_raw, col_peer(i)), piece(row_raw, col_peer(i)), S_R1, (r, col_peer(i))
                )
            )

        @pl.when(r == c)
        def _():
            each_peer(lambda i: send_to(coords_ref, col_sites, S_SITES, (row_peer(i), c)))
            col_sites[...] = coords_ref[...]

        @pl.when(r == d)
        def _():
            each_peer(lambda i: send_to(pivot_info, pivot_info, S_PIVOT, (row_peer(i), c)))

    lax.fori_loop(0, 2, half, 0)

    @pl.when((r == d) & (c == d))
    def _():
        factor_rx[8 * d : 8 * d + 8, :] = inverse[8 * d : 8 * d + 8, :]
        each_peer(
            lambda i: send_to(
                rows8(inverse, col_peer(i)), rows8(factor_rx, col_peer(i)), S_F1, (r, col_peer(i))
            )
        )

    @pl.when((r == d) & (c != d))
    def _():
        wait(rows8(factor_rx, c), recv.at[S_F1])

    @pl.when(r == d)
    def _():
        each_peer(
            lambda i: send_to(rows8(factor_rx, c), rows8(factor_rx, c), S_F2, (row_peer(i), c))
        )

    def share_row(i, carry):
        to = col_peer(2 * i)

        @pl.when(to != d)
        def _():
            send_to(piece(row_raw, c), piece(row_raw, c), S_R2, (r, to), row_recv.at[c // 2])

        return carry

    @pl.when(c != d)
    def _():
        wait(piece(row_raw, c), recv.at[S_R1])

    lax.fori_loop(1, 8, share_row, 0)

    @pl.when(sibling != d)
    def _():
        send_to(piece(row_raw, c), piece(row_raw, c), S_R3, (r, sibling))

    wait(hist_rx.at[pl.ds(1, 15)], recv.at[S_H1])
    own = pl.ds(pl.multiple_of(c * 8, 8), 8)
    summed = lax.fori_loop(1, N, lambda i, total: total + hist_rx[i], hist[own, :])
    hist_sum[...] = jnp.where(iota((8, 128), 0) < 2, summed, 0.0)
    each_peer(lambda i: send_to(hist_sum, hist_rx2.at[i], S_H2, (row_peer(i), c)))

    @pl.when(r != c)
    def _():
        wait(col_sites, recv.at[S_SITES])

    col_x = col_sites[0] * factor
    col_y = col_sites[1] * factor

    def form(a):
        def eight(q, carry):
            for u in range(8):
                t = q * 8 + u
                at = pl.ds(pl.multiple_of(a * 1024 + t * 8, 8), 8)
                value = matern(
                    coords_s[0, a, t] * factor - col_x, coords_s[1, a, t] * factor - col_y, variance
                )
                corr[at, :] = value - corr[at, :]
            return carry

        lax.fori_loop(0, 16, eight, 0)

        @pl.when(r == c)
        def _():
            tile = pl.ds(a * 1025, 128, stride=8)
            row = jnp.sum(jnp.where(iota((8, 128), 0) == a, nugget, 0.0), axis=0, keepdims=True)
            corr[tile, :] = corr[tile, :] + jnp.where(diagonal, row, 0.0)

        for b in range(8):

            @pl.when(a == b)
            def _():
                at = pl.ds(b * 1024, 1024)
                pltpu.make_async_copy(corr.at[at], matrix_out[b], out_sem).start()

    lax.fori_loop(0, EARLY, lambda a, carry: (form(a), carry)[1], 0)

    @pl.when(r != d)
    def _():
        wait(piece(col_raw, r), recv.at[S_C1])

    def share_col(i):
        @pl.when(row_peer(i) != d)
        def _():
            send_to(piece(col_raw, r), piece(col_raw, r), S_C2, (row_peer(i), c))

    each_peer(share_col)

    hist_rx[0] = hist[own, :]

    def unpack(i, found):
        source = lax.rem(c - i + N, N)
        packed = jnp.broadcast_to(hist_rx[i][2:3, :], (8, 128))
        spread = pltpu.roll(packed, 0, 1, stride=8, stride_axis=0)
        here = (lane // 8) == source
        return tuple(
            jnp.where(
                here,
                pltpu.roll(spread, lax.rem(8 * source + 64 * j + 72, 128), 1),
                found[j],
            )
            for j in range(2)
        )

    found = lax.fori_loop(0, N, unpack, (jnp.zeros((8, 128), F32), jnp.zeros((8, 128), F32)))
    found = [jnp.concatenate([x[7 - a : 8 - a] for a in range(8)], axis=0) for x in found]
    for j in range(2):
        sites_out[j] = found[j]

    @pl.when(r == d)
    def _():
        pivot_obs[...] = jnp.concatenate(
            [pick_row(found[0]), pick_row(found[1]), jnp.zeros((6, 128), F32)], axis=0
        )
        each_peer(lambda i: send_to(pivot_obs, pivot_obs, S_PO, (row_peer(i), c)))

    def pass_on(i):
        source = lax.rem(c + 16 - 2 * i, N)
        wait(piece(row_raw, source), row_recv.at[source // 2])

        @pl.when(sibling != d)
        def _():
            send_to(piece(row_raw, source), piece(row_raw, source), S_R3, (r, sibling))

    def pass_own(i):
        source = lax.rem(c + 16 - 2 * i, N)
        send_to(piece(row_raw, source), piece(row_raw, source), S_R3, (r, sibling))

    def pass_piece(i):
        @pl.when(c != d)
        def _():
            pass_on(i)

        @pl.when(c == d)
        def _():
            pass_own(i)

    def form_and_pass(a, carry):
        form(a)
        pass_piece(a - 1)
        return carry

    def later(a, carry):
        @pl.when(a == MIDDLE)
        def _():
            last_hops()

        form_and_pass(a, carry)
        return carry

    def last_hops():
        @pl.when(r != d)
        def _():
            wait(rows8(factor_rx, c), recv.at[S_F2])

        each_peer(lambda i: send_to(rows8(factor_rx, c), rows8(factor_rx, c), S_F3, (r, col_peer(i))))

        wait(hist_rx2.at[pl.ds(1, 15)], recv.at[S_H2])
        hist_all[own, :] = lax.fori_loop(
            1, N, lambda i, total: total + hist_rx2[i], hist_sum[...]
        )
        each_peer(
            lambda i: send_to(rows8(hist_all, c), rows8(hist_all, c), S_H3, (r, col_peer(i)))
        )

    lax.fori_loop(EARLY, 8, later, 0)
    pass_piece(7)

    @pl.when(r != d)
    def _():
        wait(pivot_info, recv.at[S_PIVOT])

    info = pivot_info[...]
    across = jnp.transpose(info)
    px = info[0:1, :] * factor
    py = info[1:2, :] * factor
    pnug = jnp.where(diagonal, info[2:3, :], 0.0)
    tx = across[:, 0:1] * factor
    ty = across[:, 1:2] * factor

    def panels(a, carry):
        at = pl.ds(pl.multiple_of(a * 128, 128), 128)
        turn = lax.rem(128 - a, 128)
        x = pltpu.roll(x_rows, turn, 1)[:, 0:1]
        y = pltpu.roll(y_rows, turn, 1)[:, 0:1]
        extra = jnp.where(tile_at == a, pnug, 0.0)
        rows_out[at, :] = matern(x - px, y - py, variance) + jnp.where(r == d, extra, 0.0)
        x = col_sites[0, pl.ds(a, 1), :] * factor
        y = col_sites[1, pl.ds(a, 1), :] * factor
        cols_out[a] = matern(tx - x, ty - y, variance) + jnp.where(c == d, extra, 0.0)
        return carry

    lax.fori_loop(0, 8, panels, 0)

    @pl.when(r != d)
    def _():
        wait(col_raw.at[pl.ds(0, 15 * PIECE)], recv.at[S_C2])
        wait(pivot_obs, recv.at[S_PO])


    def less_cols(b, carry):
        cols_out[b] = cols_out[b] - col_raw[pl.ds(b, 128, stride=8), :]
        return carry

    lax.fori_loop(0, 8, less_cols, 0)
    pivot_out[...] = pivot_obs[...]
    wait(factor_rx.at[pl.ds(0, 120)], recv.at[S_F3])
    inverse_out[...] = factor_rx[...]
    wait(hist_all.at[pl.ds(0, 120)], recv.at[S_H3])
    hist_out[...] = hist_all[...]

    @pl.when(c != d)
    def _():
        wait(row_raw.at[pl.ds(0, 8 * PIECE)], recv.at[S_R3])

    def less_rows(a, carry):
        at = pl.ds(pl.multiple_of(a * 128, 128), 128)
        rows_out[at, :] = rows_out[at, :] - row_raw[at, :]
        return carry

    lax.fori_loop(0, 8, less_rows, 0)

    def sent(ref, which):
        wait(ref, send.at[which])

    @pl.when(r == d)
    def _():
        sent(hist.at[pl.ds(0, 120)], S_PIVOT)
        sent(hist.at[pl.ds(0, 120)], S_F2)
        sent(hist.at[pl.ds(0, 120)], S_PO)
        sent(col_raw.at[pl.ds(0, 15 * PIECE)], S_C1)
        sent(col_raw.at[pl.ds(0, 15 * PIECE)], S_C2)

    @pl.when(r != d)
    def _():
        sent(col_raw.at[pl.ds(0, 14 * PIECE)], S_C2)

    @pl.when(r == c)
    def _():
        sent(row_raw.at[pl.ds(0, 240)], S_SITES)

    @pl.when((r == d) & (c == d))
    def _():
        sent(hist.at[pl.ds(0, 120)], S_F1)

    @pl.when(c == d)
    def _():
        sent(row_raw.at[pl.ds(0, 15 * PIECE)], S_R1)

    for which in (S_F3, S_H1, S_H2, S_H3):
        sent(hist.at[pl.ds(0, 120)], which)

    same_place = lax.rem(c, 2) == d % 2

    @pl.when(same_place & (c != d))
    def _():
        sent(row_raw.at[pl.ds(0, 6 * PIECE)], S_R2)

    @pl.when(jnp.logical_not(same_place) | (c == d))
    def _():
        sent(row_raw.at[pl.ds(0, 7 * PIECE)], S_R2)

    @pl.when(sibling != d)
    def _():
        sent(row_raw.at[pl.ds(0, 8 * PIECE)], S_R3)

    wait(corr, out_sem)


def exchange(d, *args):
    vmem = pl.BlockSpec(memory_space=pltpu.VMEM)
    hbm = pl.BlockSpec(memory_space=pl.ANY)
    far = pl.BlockSpec(memory_space=pltpu.HBM)
    shape = lambda *s: jax.ShapeDtypeStruct(s, F32)
    return pl.pallas_call(
        functools.partial(exchange_kernel, d),
        out_shape=(
            *[shape(1024, 128) for _ in range(KEPT)],
            *[pltpu.HBM((1024, 128), F32) for _ in range(8 - KEPT)],
            shape(1024, 128),
            shape(8, 128, 128),
            shape(128, 128),
            shape(128, 128),
            shape(2, 8, 128),
            shape(8, 128),
        ),
        in_specs=[hbm] * 10,
        out_specs=(vmem,) * KEPT + (far,) * (8 - KEPT) + (vmem,) * 6,
        scratch_shapes=[
            pltpu.SMEM((1,), I32),
            pltpu.SMEM((NREG,), F32),
            pltpu.SMEM((1,), F32),
            pltpu.SMEM((1,), F32),
            pltpu.SMEM((2, 8, 128), F32),
            pltpu.VMEM((2, 8, 128), F32),
            pltpu.VMEM((8, 128), I32),
            pltpu.VMEM((8, 8), I32),
            pltpu.VMEM((8, 8), F32),
            pltpu.VMEM((8, 8), F32),
            pltpu.VMEM((8192, 128), F32),
            pltpu.VMEM((1024, 128), F32),
            pltpu.VMEM((1024, 128), F32),
            pltpu.VMEM((128, 128), F32),
            pltpu.VMEM((128, 128), F32),
            pltpu.VMEM((128, 128), F32),
            pltpu.VMEM((2, 8, 128), F32),
            pltpu.VMEM((8, 128), F32),
            pltpu.VMEM((128, 128), F32),
            pltpu.VMEM((N, 8, 128), F32),
            pltpu.VMEM((8, 128), F32),
            pltpu.VMEM((N, 8, 128), F32),
            pltpu.VMEM((128, 128), F32),
            pltpu.VMEM((8, 128), F32),
            pltpu.SemaphoreType.DMA,
            pltpu.SemaphoreType.DMA((10,)),
            pltpu.SemaphoreType.DMA,
            pltpu.SemaphoreType.DMA((15,)),
            pltpu.SemaphoreType.DMA((15,)),
            pltpu.SemaphoreType.DMA((8,)),
        ],
        compiler_params=pltpu.CompilerParams(
            collective_id=d, has_side_effects=True, vmem_limit_bytes=12 * MIB
        ),
        name="exchange",
    )(*args)


def quantile(x):
    w = -jnp.log((1.0 - x) * (1.0 + x)) - 2.5
    p = jnp.full_like(w, 2.81022636e-08)
    for coefficient in (
        3.43273939e-07,
        -3.5233877e-06,
        -4.39150654e-06,
        0.00021858087,
        -0.00125372503,
        -0.00417768164,
        0.246640727,
        1.50140941,
    ):
        p = coefficient + p * w
    return p * x


def update_kernel(k_ref, *refs):
    matrix_ref = refs[:8]
    rows_ref, cols_ref, inverse_ref, hist_ref, sites_ref, pivot_ref = refs[8:14]
    trailing_hbm, panel_hbm, scores_ref, terms_ref = refs[14:18]
    trailing, panel, late, in_sem, out_sem, panel_sem = refs[18:]
    loads = [
        pltpu.make_async_copy(matrix_ref[a], late.at[a - KEPT], in_sem.at[a - KEPT])
        for a in range(KEPT, 8)
    ]
    for load in loads:
        load.start()
    inverse = inverse_ref[...]
    cols = dot3(inverse, jnp.concatenate([cols_ref[b] for b in range(8)], axis=1), NN)
    high, low = split2(cols)
    right = jnp.concatenate([high, low, high], axis=0)
    whole = dot3(rows_ref[...], inverse, NT)
    panel[...] = whole
    whole_high, whole_low = split2(whole)
    left = jnp.concatenate([whole_high, whole_high, whole_low], axis=1)

    counts = hist_ref[...]
    level = iota((128, 128), 0)
    across = iota((128, 128), 1)
    parts = split3(counts)
    ahead = (across < level).astype(F32).astype(BF16)
    earlier = (level < across).astype(F32).astype(BF16)
    above = jnp.zeros((128, 128), F32)
    along = jnp.zeros((128, 128), F32)
    for part in parts:
        above = above + lax.dot_general(ahead, part, NN, preferred_element_type=F32)
        along = along + lax.dot_general(part, earlier, NN, preferred_element_type=F32)
    before = jnp.sum(above, axis=1, keepdims=True) + along
    total = jnp.sum(jnp.sum(counts, axis=1, keepdims=True), axis=0, keepdims=True)

    bins_f = jnp.concatenate([sites_ref[0], pivot_ref[...]], axis=0)
    fraction = jnp.concatenate([sites_ref[1], pivot_ref[...]], axis=0)
    bins_i = bins_f.astype(I32)
    high_i = (bins_i // 256) * 8 + (bins_i // 128) % 2
    low_i = bins_i % 128
    high_hot = jnp.concatenate(
        [(level == high_i[i : i + 1, :]).astype(F32).astype(BF16) for i in range(9)], axis=1
    )
    tripled = jnp.concatenate([high_hot] * 3, axis=0)
    look = [
        lax.dot_general(
            jnp.concatenate(split3(table), axis=0), tripled, TN, preferred_element_type=F32
        )
        for table in (before, counts)
    ]
    probs = []
    for i in range(9):
        hot = level == low_i[i : i + 1, :]
        at = slice(i * 128, (i + 1) * 128)
        start = jnp.sum(jnp.where(hot, look[0][:, at], 0.0), axis=0, keepdims=True)
        count = jnp.sum(jnp.where(hot, look[1][:, at], 0.0), axis=0, keepdims=True)
        part = fraction[i : i + 1, :] if i < 8 else fraction[9:10, :]
        probs.append((start + part * count) / total)
    probs = jnp.concatenate(probs + [jnp.full((7, 128), 0.5, F32)], axis=0)
    found = ROOT_TWO * quantile(2.0 * jnp.clip(probs, 0.01, 0.99) - 1.0)
    z = dot3(jnp.broadcast_to(found[8:9, :], (8, 128)), inverse, NT)
    diagonal = jnp.sum(jnp.where(level == across, inverse, 0.0), axis=0, keepdims=True)
    terms_ref[0] = -2.0 * jnp.sum(jnp.log(diagonal))
    terms_ref[1] = jnp.sum(z[0:1, :] * z[0:1, :])
    moved = dot3(z, whole, NT)
    k = k_ref[0]
    here = lax.axis_index("row") == k % N
    for a in range(8):
        score = found[a : a + 1, :] - moved[0:1, a * 128 : (a + 1) * 128]
        scores_ref[a : a + 1, :] = jnp.where(here & (k // N == a), z[0:1, :], score)

    panel_copy = pltpu.make_async_copy(panel, panel_hbm, panel_sem)
    panel_copy.start()
    for a in range(8):
        change = lax.dot_general(
            left[a * 128 : (a + 1) * 128], right, NN, preferred_element_type=F32
        )
        block = matrix_ref[a] if a < KEPT else late.at[a - KEPT]
        if a >= KEPT:
            loads[a - KEPT].wait()
        for b in range(8):
            at = pl.ds(a * 1024 + b, 128, stride=8)
            before = block[pl.ds(b, 128, stride=8), :]
            trailing[at, :] = before - change[:, b * 128 : (b + 1) * 128]
        at = pl.ds(a * 1024, 1024)
        pltpu.make_async_copy(trailing.at[at], trailing_hbm.at[at], out_sem.at[a]).start()

    panel_copy.wait()
    for a in range(8):
        at = pl.ds(a * 1024, 1024)
        pltpu.make_async_copy(trailing.at[at], trailing_hbm.at[at], out_sem.at[a]).wait()


def update(*args):
    shape = lambda *s: jax.ShapeDtypeStruct(s, F32)
    vmem = pl.BlockSpec(memory_space=pltpu.VMEM)
    smem = pl.BlockSpec(memory_space=pltpu.SMEM)
    hbm = pl.BlockSpec(memory_space=pl.ANY)
    far = pl.BlockSpec(memory_space=pltpu.HBM)
    return pl.pallas_call(
        update_kernel,
        out_shape=(shape(8192, 128), shape(1024, 128), shape(8, 128), shape(2)),
        in_specs=[smem] + [vmem] * KEPT + [far] * (8 - KEPT) + [vmem] * 6,
        out_specs=(hbm, hbm, vmem, smem),
        scratch_shapes=[
            pltpu.VMEM((8192, 128), F32),
            pltpu.VMEM((1024, 128), F32),
            pltpu.VMEM((8 - KEPT, 1024, 128), F32),
            pltpu.SemaphoreType.DMA((8 - KEPT,)),
            pltpu.SemaphoreType.DMA((8,)),
            pltpu.SemaphoreType.DMA,
        ],
        compiler_params=pltpu.CompilerParams(vmem_limit_bytes=12 * MIB),
        name="update",
    )(*args)


def on_device(
    panel_index,
    coords,
    region_ids,
    nugget,
    variance,
    length,
    correction,
    bin_index,
    fraction,
    weights,
):
    coords = coords.reshape(2, 8, 128)
    args = (
        panel_index,
        nugget,
        variance,
        length,
        coords,
        region_ids.reshape(8, 128),
        bin_index.reshape(8, 8),
        fraction.reshape(8, 8),
        weights.reshape(8, 8),
        correction.reshape(8192, 128),
    )
    branches = [functools.partial(exchange, d) for d in range(N)]
    moved = lax.switch(panel_index[0] & (N - 1), branches, *args)
    trailing, panel, scores, terms = update(panel_index, *moved)
    return (
        trailing.reshape(8, 1, 128, 8, 1, 128),
        panel.reshape(8, 1, 128, 128),
        scores.reshape(8, 1, 128),
        terms,
    )


def solution(mesh):
    in_specs = (
        P(),
        P(None, None, "row", None),
        P(None, "row", None),
        P(),
        P(),
        P(),
        P(None, "row", None, None, "col", None),
        P(None, "row", "col", None),
        P(None, "row", "col", None),
        P(None, "row", "col", None),
    )
    out_specs = (
        P(None, "row", None, None, "col", None),
        P(None, "row", None, None),
        P(None, "row", None),
        P(),
    )
    return jax.shard_map(
        on_device, mesh=mesh, in_specs=in_specs, out_specs=out_specs, check_vma=False
    )
```
